32 devices in a mesh: section: 4 (over y, x), space: 8 (over z, core).
Axes of the slice: x: 2, y: 2, z: 4, core: 2. Of those that a mesh axis runs over, the one named last changes fastest.
Arguments:
- raster: bfloat16 [4, 32, 128, 256], P(None, 'space'), may hold values from -6 to 6
- row_coef: bfloat16 [4, 15, 32, 128], P('section', None, 'space'), may hold values from -1.5 to 1.5
- col_coef: bfloat16 [4, 15, 128, 32], P('section', None, 'space'), may hold values from -1.5 to 1.5
- norm_gain: bfloat16 [4, 256], P('section'), may hold values from 0.099609375 to 1.8984375
- weight_in: bfloat16 [4, 256, 512], P('section'), may hold values from -0.375 to 0.375
- bias_in: bfloat16 [4, 512], P('section'), may hold values from -3 to 3
- weight_out: bfloat16 [4, 512, 256], P('section'), may hold values from -0.25 to 0.25
- readout: bfloat16 [256], replicated, may hold values from -0.375 to 0.375
Outputs:
- density: float32 [4, 32, 128], P('section', 'space')
The draws below stay inside these ranges and needn't reach their ends.
All inputs are finite; a program needn't handle non-finite values.
Results may differ from the reference program's by a relative error of at most 0.015.
Values may be sent and summed in bfloat16 or wider, within the bound.
No kernel may reach another device: no remote copies, remote signals or barrier semaphores. Data moves between devices by JAX's collectives and lax.ppermute only.
A program may use at most 64 MiB of HBM per device.

```python
import jax
import jax.numpy as jnp
from jax import lax

CHANNELS = 256
HIDDEN_SIZE = 512
TAPS = 15
W = 128
H = 32
LAYERS = 4
WINDOWS = 4


def steps_of(own_key, extent, shards, low, largest):
    level, own = 1.0, jax.random.fold_in(own_key, 6)
    for position, shards_of in shards:
        steps = jnp.exp(jax.random.uniform(jax.random.fold_in(own, position), (shards_of,), jnp.float32, low / len(shards), largest / len(shards)))
        level = level * jnp.repeat(steps, extent[position] // shards_of).reshape([-1 if axis == position else 1 for axis in range(len(extent))])
    return level


def centred(stream_key, dims, deviation, reach, shards=(), kind=jnp.bfloat16):
    array = deviation * jax.random.normal(stream_key, dims, jnp.float32)
    if shards:
        array = array * steps_of(stream_key, dims, shards, -0.22, 0.18)
    return jnp.clip(array, -reach, reach).astype(kind)


def setup_inputs(seed: int = 0) -> dict:
    key_list = jax.random.split(jax.random.key(seed), 9)
    raster = centred(key_list[0], (WINDOWS, H, W, CHANNELS), 1.0, 6.0, ((1, 8),))
    row_coef = centred(key_list[1], (LAYERS, TAPS, H, W), TAPS ** -0.5, 1.5, ((0, 4), (2, 8)))
    col_coef = centred(key_list[2], (LAYERS, TAPS, W, H), TAPS ** -0.5, 1.5, ((0, 4), (2, 8)))
    norm_gain = jnp.clip(1.0 + 0.18 * jax.random.normal(key_list[3], (LAYERS, CHANNELS), jnp.float32), 0.099609375, 1.8984375).astype(jnp.bfloat16)
    weight_in = centred(key_list[4], (LAYERS, CHANNELS, HIDDEN_SIZE), CHANNELS ** -0.5, 0.375, ((0, 4),))
    bias_in = centred(key_list[5], (LAYERS, HIDDEN_SIZE), 0.5, 3.0, ((0, 4),))
    weight_out = centred(key_list[6], (LAYERS, HIDDEN_SIZE, CHANNELS), HIDDEN_SIZE ** -0.5, 0.25, ((0, 4),))
    readout = centred(key_list[7], (CHANNELS,), CHANNELS ** -0.5, 0.375)
    return {"raster": raster, "row_coef": row_coef, "col_coef": col_coef, "norm_gain": norm_gain, "weight_in": weight_in, "bias_in": bias_in, "weight_out": weight_out, "readout": readout}


def row_stencil(surface, coefficients):
    taps_count = coefficients.shape[0]
    radius = taps_count // 2
    columns = surface.shape[1]
    padded = jnp.pad(surface.astype(jnp.float32), ((0, 0), (radius, radius), (0, 0)))
    summed = jnp.zeros(surface.shape, jnp.float32)
    for offset in range(taps_count):
        summed = summed + coefficients[offset].astype(jnp.float32)[:, :, None] * padded[:, offset:offset + columns, :]
    return summed

def col_stencil(surface, coefficients):
    taps_count = coefficients.shape[0]
    radius = taps_count // 2
    lines = surface.shape[0]
    swapped = jnp.swapaxes(coefficients, 1, 2)
    padded = jnp.pad(surface.astype(jnp.float32), ((radius, radius), (0, 0), (0, 0)))
    summed = jnp.zeros(surface.shape, jnp.float32)
    for offset in range(taps_count):
        summed = summed + swapped[offset].astype(jnp.float32)[:, :, None] * padded[offset:offset + lines, :, :]
    return summed

def dense_part(mixed_field, norm_gain, weight_in, bias_in, weight_out):
    inverse = lax.rsqrt(lax.optimization_barrier(jnp.mean(mixed_field * mixed_field, axis=-1, keepdims=True)) + 1e-06)
    normed = (mixed_field * inverse * norm_gain.astype(jnp.float32)).astype(jnp.bfloat16)
    hidden = jax.nn.gelu(jnp.dot(normed, weight_in, preferred_element_type=jnp.float32) + bias_in.astype(jnp.float32), approximate=True).astype(jnp.bfloat16)
    return (mixed_field + jnp.dot(hidden, weight_out, preferred_element_type=jnp.float32)).astype(jnp.bfloat16)

def reference(raster, row_coef, col_coef, norm_gain, weight_in, bias_in, weight_out, readout):

    def one_window(surface):
        for layer_index in range(LAYERS):
            row_part = row_stencil(surface, row_coef[layer_index]).astype(jnp.bfloat16)
            mixed_field = col_stencil(row_part, col_coef[layer_index])
            surface = dense_part(mixed_field, norm_gain[layer_index], weight_in[layer_index], bias_in[layer_index], weight_out[layer_index])
        logits = jnp.dot(surface, readout, preferred_element_type=jnp.float32)
        return jax.nn.softplus(logits)
    return lax.map(one_window, raster)
```

```python
import functools

import jax
import jax.numpy as jnp
from jax import lax
from jax.experimental import pallas as pl
from jax.experimental.pallas import tpu as pltpu
from jax.sharding import PartitionSpec as P

F32 = jnp.float32
BF16 = jnp.bfloat16
VMEM = pl.BlockSpec(memory_space=pltpu.VMEM)
SMEM = pl.BlockSpec(memory_space=pltpu.SMEM)
ANY = pl.BlockSpec(memory_space=pl.ANY)


def from_behind(array, axis, by):
    size = lax.axis_size(axis)
    pairs = [(i, i + by) for i in range(size) if 0 <= i + by < size]
    return lax.ppermute(array, axis, pairs)


def from_root(value, axis, source):
    kept = jnp.where(lax.axis_index(axis) == source, value, 0).astype(value.dtype)
    return lax.psum(kept, axis)


def row_stencil(surface, coefficients):
    taps_count = coefficients.shape[0]
    radius = taps_count // 2
    columns = surface.shape[1]
    padded = jnp.pad(surface.astype(F32), ((0, 0), (radius, radius), (0, 0)))
    summed = jnp.zeros(surface.shape, F32)
    for offset in range(taps_count):
        summed = (
            summed
            + coefficients[offset].astype(F32)[:, :, None] * padded[:, offset : offset + columns, :]
        )
    return summed


def col_stencil(surface, coefficients):
    taps_count = coefficients.shape[0]
    radius = taps_count // 2
    lines = surface.shape[0]
    swapped = jnp.swapaxes(coefficients, 1, 2)
    padded = jnp.pad(surface.astype(F32), ((radius, radius), (0, 0), (0, 0)))
    summed = jnp.zeros(surface.shape, F32)
    for offset in range(taps_count):
        summed = (
            summed
            + swapped[offset].astype(F32)[:, :, None] * padded[offset : offset + lines, :, :]
        )
    return summed


def apply_layer(current, params):
    row_part = row_stencil(current, params[0]).astype(BF16)
    columns_view = lax.all_to_all(row_part, "space", split_axis=1, concat_axis=0, tiled=True)
    mixed_field = col_stencil(columns_view, params[1])
    inverse = lax.rsqrt(jnp.mean(mixed_field * mixed_field, axis=-1, keepdims=True) + 1e-06)
    normed = (mixed_field * inverse * params[2].astype(F32)).astype(BF16)
    hidden = jax.nn.gelu(
        jnp.dot(normed, params[3], preferred_element_type=F32) + params[4].astype(F32),
        approximate=True,
    ).astype(BF16)
    return (mixed_field + jnp.dot(hidden, params[5], preferred_element_type=F32)).astype(BF16)


def to_rows(output):
    return lax.all_to_all(output, "space", split_axis=0, concat_axis=1, tiled=True)


def read_density(output, readout):
    return jax.nn.softplus(jnp.dot(output, readout, preferred_element_type=F32))


def layers_over_sections(
    raster, row_coef, col_coef, norm_gain, weight_in, bias_in, weight_out, readout
):
    sections = lax.axis_size("section")
    spaces = lax.axis_size("space")
    windows = raster.shape[0]
    position = lax.axis_index("section")
    params = (row_coef[0], col_coef[0], norm_gain[0], weight_in[0], bias_in[0], weight_out[0])
    carried = jnp.zeros(raster.shape[1:], BF16)
    finished = jnp.zeros((windows, raster.shape[1] * spaces, raster.shape[2] // spaces), F32)
    for moment in range(windows + sections - 1):
        entering = raster[min(moment, windows - 1)]
        current = jnp.where(position == 0, entering, carried)
        output = apply_layer(current, params)
        finished_index = moment - (sections - 1)
        if finished_index >= 0:
            finished = finished.at[finished_index].set(read_density(output, readout))
        if moment < windows + sections - 2:
            carried = from_behind(to_rows(output), "section", 1)
    row_density = lax.all_to_all(finished, "space", split_axis=1, concat_axis=2, tiled=True)
    everyone = from_root(row_density, "section", sections - 1)
    return lax.dynamic_slice_in_dim(everyone, position, 1, 0)


TAPS = 15
RADIUS = 7
ROWS = 32
COLS = 16
WIDE = 128
CELLS = ROWS * COLS
GROUP = 8 * COLS


def call(kernel, outs, specs, scratch=(), cost=1000):
    return pl.pallas_call(
        kernel,
        out_shape=outs,
        in_specs=specs,
        out_specs=jax.tree.map(lambda _: VMEM, outs),
        scratch_shapes=list(scratch),
        compiler_params=pltpu.CompilerParams(vmem_limit_bytes=48 * 1024 * 1024),
        cost_estimate=pl.CostEstimate(flops=cost * 1000, bytes_accessed=cost, transcendentals=0),
    )


def shaped(shape, kind=BF16):
    return jax.ShapeDtypeStruct(shape, kind)


def iota(shape, axis):
    return lax.broadcasted_iota(jnp.int32, shape, axis)


def picked(which, values):
    out = values[0]
    for k in range(1, len(values)):
        out = jnp.where(which == k, values[k], out)
    return out


def row0_kernel(place, q0, q1, q2, q3, own, sib, o0, o1, o2, o3, chunk):
    s, c, z = place[0], place[1], place[2]
    lane, line = iota((WIDE, WIDE), 1), iota((WIDE, WIDE), 0)
    source = line + lane - RADIUS
    inside = (lane < TAPS) & (source >= 0) & (source < WIDE)
    for i in range(8):
        taps = picked(s, [q[i].astype(F32) for q in (q0, q1, q2, q3)])
        spread = jnp.concatenate([jnp.transpose(taps), jnp.zeros((WIDE, WIDE - 16), F32)], 1)
        spread = jnp.where(inside, spread, 0.0)
        band = pltpu.roll(spread, WIDE - RADIUS, 1, stride=1, stride_axis=0).astype(BF16)
        cells = jnp.where(c == i // 4, own[i % 4], sib[i % 4])
        done = jnp.dot(band, cells, preferred_element_type=F32)
        done = done.reshape(4, 2, COLS, done.shape[-1])
        done = jnp.where(c == 0, done[:, 0], done[:, 1]).astype(BF16)
        chunk[:, COLS * i : COLS * (i + 1), :] = done
    for k, out in enumerate((o0, o1, o2, o3)):
        out[...] = chunk[z ^ k]


def spread_kernel(place, q0, q1, q2, q3, o0, o1, o2, o3, chunk):
    c, z = place[1], place[2]
    for i in range(4):
        stacked = jnp.concatenate([q[r].astype(F32) for r in (i, i + 4) for q in (q0, q1, q2, q3)], 0)
        turned = jnp.transpose(stacked).reshape(4, 2, COLS, WIDE)
        chunk[:, COLS * i : COLS * (i + 1), :] = jnp.where(c == 0, turned[:, 0], turned[:, 1]).astype(BF16)
    for k, out in enumerate((o0, o1, o2, o3)):
        out[...] = chunk[z ^ k]


def prepare_cols_kernel(layers, place, q0, q1, q2, q3, *rest):
    outs, (turned, ordered) = rest[: len(layers)], rest[len(layers) :]
    s = place[0]
    tap_in, tap_out = iota((WIDE, 256), 0), iota((WIDE, 256), 1)
    expand = jnp.where((tap_in == tap_out // COLS) & (tap_in < TAPS), 1.0, 0.0).astype(BF16)
    lane, line = iota((COLS, 256), 1), iota((COLS, 256), 0)
    same = line == lane % COLS
    for layer, out in zip(layers, outs):
        for m in range(4):
            taps = picked(s ^ layer, [q[8 + m].astype(F32) for q in (q0, q1, q2, q3)])
            turned[128 * m : 128 * (m + 1), :] = jnp.concatenate(
                [jnp.transpose(taps), jnp.zeros((128, WIDE - 16), F32)], 1
            )
        for i in range(ROWS):
            ordered[COLS * i : COLS * (i + 1), :] = turned[pl.ds(i, COLS, stride=ROWS), :]
        wide = jnp.dot(ordered[...].astype(BF16), expand, preferred_element_type=F32)
        for i in range(ROWS):
            row = i + lane // COLS - RADIUS
            block = jnp.where(same & (row >= 0) & (row < ROWS), wide[COLS * i : COLS * (i + 1)], 0.0)
            block = jnp.concatenate([block, jnp.zeros((COLS, CELLS - 256), F32)], 1)
            shift = (COLS * (i - RADIUS)) % CELLS
            if shift:
                block = pltpu.roll(block, shift, 1)
            out[COLS * i : COLS * (i + 1), :] = block.astype(BF16)


def prepare_rows_kernel(layers, place, g0, g1, g2, g3, *rest):
    outs, (parts,) = rest[: len(layers)], rest[len(layers) :]
    s, c, z, p = place[0], place[1], place[2], place[3]
    last = place[4]
    for k, g in enumerate((g0, g1, g2, g3)):
        parts[z ^ k] = g[...].astype(F32)
    lane, line = iota((GROUP, WIDE), 1), iota((GROUP, WIDE), 0)
    source = line % COLS + lane - RADIUS
    tap = lane < TAPS
    own_mask = tap & (source >= 0) & (source < COLS)
    left_mask = tap & (source < 0) & (p > 0)
    right_mask = tap & (source >= COLS) & (p < last)
    for layer, out in zip(layers, outs):
        kk = s ^ layer
        for g in range(4):
            part = parts[g]
            low = pltpu.roll(part, (WIDE - 16 * kk) % WIDE, 1)
            high = pltpu.roll(part, (WIDE + 64 - 16 * kk) % WIDE, 1)
            taps = jnp.concatenate([low, high], 0)
            own = jnp.where(own_mask, taps, 0.0)
            own = pltpu.roll(own, WIDE - RADIUS, 1, stride=1, stride_axis=0)
            left = jnp.where(left_mask, taps, 0.0)
            right = jnp.where(right_mask, taps, 0.0)
            lefts, rights = [], []
            for i in range(8):
                cut = slice(COLS * i, COLS * (i + 1))
                lefts.append(pltpu.roll(left[cut], 8 * i + 1, 1, stride=1, stride_axis=0))
                rights.append(pltpu.roll(right[cut], (8 * i - 23) % WIDE, 1, stride=1, stride_axis=0))
            left, right = jnp.concatenate(lefts, 0), jnp.concatenate(rights, 0)
            sides = jnp.where(
                c == 0, right + pltpu.roll(left, 64, 1), left + pltpu.roll(right, 64, 1)
            )
            out[g, :, 0:WIDE] = own.astype(BF16)
            out[g, :, WIDE : 2 * WIDE] = sides.astype(BF16)


def fetch(which, sources, buffer, sem):
    for k in range(4):

        @pl.when(which == k)
        def _():
            pltpu.make_async_copy(sources[k], buffer, sem).start()


def layer_kernel(layer, final, place, x, n0, n1, n2, rows_band, cols_band, readout, *rest):
    mine, theirs, rest = rest[0:4], rest[4:8], rest[8:]
    if final:
        (density,), (field, weights, sems) = rest[:1], rest[1:]
    else:
        (out, to_core, to_z), (field, weights, sems) = rest[:3], rest[3:]
    s, c, z = place[0], place[1], place[2]
    fetch(s ^ layer, mine, weights.at[0], sems.at[0])
    fetch(s ^ layer, theirs, weights.at[1], sems.at[1])
    if layer == 0:
        for k, n in enumerate((x, n0, n1, n2)):
            field[pl.ds(pl.multiple_of((z ^ k) * GROUP, GROUP), GROUP), :] = n[...]
    else:
        for g in range(4):
            cells = jnp.concatenate(
                [x[GROUP * g : GROUP * (g + 1)], n0[64 * g : 64 * (g + 1)], n1[64 * g : 64 * (g + 1)]], 0
            )
            field[GROUP * g : GROUP * (g + 1), :] = jnp.dot(
                rows_band[g], cells, preferred_element_type=F32
            ).astype(BF16)
    blocks = 2
    size = CELLS // blocks
    mixed = [
        jnp.dot(cols_band[size * b : size * (b + 1), :], field[...], preferred_element_type=F32)
        for b in range(blocks)
    ]
    pltpu.make_async_copy(mine[0], weights.at[0], sems.at[0]).wait()
    pltpu.make_async_copy(theirs[0], weights.at[1], sems.at[1]).wait()
    channels = x.shape[-1]
    gain = weights[0, 512:528, :].astype(F32)[1:2]
    for b in range(blocks):
        total = mixed[b]
        inverse = lax.rsqrt(jnp.mean(total * total, axis=-1, keepdims=True) + 1e-06)
        normed = (total * inverse * gain).astype(BF16)
        parts = []
        for half in range(2):
            bias = weights[half, 512:528, :].astype(F32)[0:1]
            hidden = jnp.dot(normed, weights[half, 0:256, :], preferred_element_type=F32) + bias
            hidden = jax.nn.gelu(hidden, approximate=True).astype(BF16)
            parts.append(jnp.dot(hidden, weights[half, 256:512, :], preferred_element_type=F32))
        total = total + (parts[0] + parts[1])
        if final:
            reader = jnp.broadcast_to(readout[...], (8, channels))
            logit = lax.dot_general(
                reader, total.astype(BF16), (((1,), (1,)), ((), ())), preferred_element_type=F32
            )
            density[:, size * b : size * (b + 1)] = (
                jnp.maximum(logit, 0.0) + jnp.log1p(jnp.exp(-jnp.abs(logit)))
            )
        else:
            out[size * b : size * (b + 1), :] = total.astype(BF16)
            cells = total.reshape(size // COLS, 2, 8, channels)
            left, right = cells[:, 0], cells[:, 1]
            cut = slice(size // 2 * b, size // 2 * (b + 1))
            to_core[cut, :] = jnp.where(c == 0, right, left).reshape(size // 2, channels).astype(BF16)
            to_z[cut, :] = jnp.where(c == 0, left, right).reshape(size // 2, channels).astype(BF16)


def gather_kernel(place, g0, g1, g2, g3, out, parts):
    z, p = place[2], place[3]
    for k, g in enumerate((g0, g1, g2, g3)):
        parts[z ^ k] = g[...]
    cells = jnp.concatenate([parts[g] for g in range(4)], 0)
    cells = pltpu.roll(cells, (CELLS - 64 * p) % CELLS, 1)[:, 0:WIDE]
    lane, line = iota((8, WIDE), 1), iota((8, WIDE), 0)
    mask = lane // COLS == line
    cells = pltpu.roll(cells, 0, 1, stride=COLS, stride_axis=0)
    for t in range(4):
        moved = pltpu.roll(cells, WIDE - COLS * t, 1) if t else cells
        out[0, t : t + 1, :] = jnp.sum(jnp.where(mask, moved, 0.0), axis=0, keepdims=True)


def window_on_section(raster, row_coef, col_coef, norm_gain, weight_in, bias_in, weight_out, readout):
    s, p = lax.axis_index("section"), lax.axis_index("space")
    c, z = p % 2, p // 2
    channels = raster.shape[-1]
    spaces = lax.axis_size("space")
    place = jnp.stack([s, c, z, p, jnp.int32(spaces - 1), s, s, s]).astype(jnp.int32)

    def core(array):
        return lax.ppermute(array, "space", [(i, i ^ 1) for i in range(spaces)])

    def chip(array, k):
        return lax.ppermute(array, "space", [(i, i ^ (2 * k)) for i in range(spaces)])

    def section(array, k):
        return lax.ppermute(array, "section", [(i, i ^ k) for i in range(4)])

    def beside(array):
        pairs = []
        for a in range(4):
            for q in range(spaces):
                other = q - 1 if q % 2 == 0 else q + 1
                to = a * spaces + other if 0 <= other < spaces else (a ^ 1) * spaces + q
                pairs.append((a * spaces + q, to))
        return lax.ppermute(array, ("section", "space"), pairs)

    rc = row_coef[0]
    rc_sib = core(rc)
    rc8 = jnp.where(c == 0, jnp.concatenate([rc, rc_sib], 1), jnp.concatenate([rc_sib, rc], 1))
    cc4 = col_coef[0].reshape(TAPS, 4, WIDE)
    pack = jnp.swapaxes(jnp.concatenate([rc8, cc4], 1), 0, 1)
    pack = jnp.pad(pack, ((0, 0), (0, 1), (0, 0)))
    packs = [pack] + [section(pack, k) for k in (1, 2, 3)]

    window = lax.dynamic_index_in_dim(raster, s, 0, keepdims=False)
    window_sib = core(window)

    def half(core_index):
        start = core_index * 256
        win = lax.dynamic_slice_in_dim(weight_in[0], start, 256, 1)
        wout = lax.dynamic_slice_in_dim(weight_out[0], start, 256, 0)
        bias = lax.dynamic_slice_in_dim(bias_in, start, 256, 1)
        return jnp.concatenate([win, wout, bias, norm_gain, jnp.zeros((14, 256), BF16)], 0)

    mine0, theirs0 = half(c), half(1 - c)
    mine = [mine0] + [section(mine0, k) for k in (1, 2, 3)]
    theirs = [theirs0] + [core(m) for m in mine[1:]]

    chunks = call(
        row0_kernel,
        (shaped((GROUP, channels)),) * 4,
        [SMEM] + [VMEM] * 6,
        [pltpu.VMEM((4, GROUP, channels), BF16)],
    )(place, *packs, window, window_sib)
    chunks = [chunks[0]] + [chip(chunks[k], k) for k in (1, 2, 3)]

    bands0 = call(
        functools.partial(prepare_cols_kernel, (0,)),
        (shaped((CELLS, CELLS)),),
        [SMEM] + [VMEM] * 4,
        [pltpu.VMEM((CELLS, WIDE), F32), pltpu.VMEM((CELLS, WIDE), F32)],
    )(place, *packs)
    spread = call(
        spread_kernel,
        (shaped((64, WIDE)),) * 4,
        [SMEM] + [VMEM] * 4,
        [pltpu.VMEM((4, 64, WIDE), BF16)],
    )(place, *packs)
    spread = [spread[0]] + [chip(spread[k], k) for k in (1, 2, 3)]
    bands = call(
        functools.partial(prepare_cols_kernel, (1, 2, 3)),
        (shaped((CELLS, CELLS)),) * 3,
        [SMEM] + [VMEM] * 4,
        [pltpu.VMEM((CELLS, WIDE), F32), pltpu.VMEM((CELLS, WIDE), F32)],
    )(place, *packs)
    cols_band = list(bands0) + list(bands)
    rows_band = [None] + list(
        call(
            functools.partial(prepare_rows_kernel, (1, 2, 3)),
            (shaped((4, GROUP, 256)),) * 3,
            [SMEM] + [VMEM] * 4,
            [pltpu.VMEM((4, 64, WIDE), F32)],
        )(place, *spread)
    )

    reader = readout.reshape(1, channels)
    for layer in range(4):
        final = layer == 3
        if layer == 0:
            fields = list(chunks)
            band = jnp.zeros((8, WIDE), BF16)
        else:
            fields = [state, core(to_core), beside(to_z), jnp.zeros((8, WIDE), BF16)]
            band = rows_band[layer]
        outs = (
            (shaped((8, CELLS), F32),)
            if final
            else (shaped((CELLS, channels)), shaped((CELLS // 2, channels)), shaped((CELLS // 2, channels)))
        )
        result = call(
            functools.partial(layer_kernel, layer, final),
            outs,
            [SMEM] + [VMEM] * 7 + [ANY] * 8,
            [
                pltpu.VMEM((CELLS, channels), BF16),
                pltpu.VMEM((2, 528, 256), BF16),
                pltpu.SemaphoreType.DMA((2,)),
            ],
        )(place, *fields, band, cols_band[layer], reader, *mine, *theirs)
        if not final:
            state, to_core, to_z = result

    density = result[0][0:1]
    density_sib = core(density)
    pair = jnp.where(
        c == 0, jnp.concatenate([density, density_sib], 0), jnp.concatenate([density_sib, density], 0)
    )
    pairs = [pair] + [chip(pair, k) for k in (1, 2, 3)]
    return call(
        gather_kernel,
        shaped((1, 4, WIDE), F32),
        [SMEM] + [VMEM] * 4,
        [pltpu.VMEM((4, 2, CELLS), F32)],
    )(place, *pairs)


def on_device(raster, row_coef, *rest):
    fits = (
        lax.axis_size("section") == 4
        and lax.axis_size("space") == 8
        and raster.shape == (4, 4, WIDE, 256)
        and row_coef.shape[1] == TAPS
    )
    plan = window_on_section if fits else layers_over_sections
    return plan(raster, row_coef, *rest)


def solution(mesh):
    placed = (
        P(None, "space", None, None),
        P("section", None, "space", None),
        P("section", None, "space", None),
        P("section", None),
        P("section", None, None),
        P("section", None),
        P("section", None, None),
        P(),
    )
    return jax.shard_map(
        on_device,
        mesh=mesh,
        in_specs=placed,
        out_specs=P("section", "space", None),
        check_vma=False,
    )
```

```python
import functools

import jax
import jax.numpy as jnp
from jax import lax
from jax.experimental import pallas as pl
from jax.experimental.pallas import tpu as pltpu
from jax.sharding import PartitionSpec as P

F32 = jnp.float32
BF16 = jnp.bfloat16
VMEM = pl.BlockSpec(memory_space=pltpu.VMEM)
ANY = pl.BlockSpec(memory_space=pl.ANY)


def from_behind(array, axis, by):
    size = lax.axis_size(axis)
    pairs = [(i, i + by) for i in range(size) if 0 <= i + by < size]
    return lax.ppermute(array, axis, pairs)


def from_root(value, axis, source):
    kept = jnp.where(lax.axis_index(axis) == source, value, 0).astype(value.dtype)
    return lax.psum(kept, axis)


def row_stencil(surface, coefficients):
    taps_count = coefficients.shape[0]
    radius = taps_count // 2
    columns = surface.shape[1]
    padded = jnp.pad(surface.astype(F32), ((0, 0), (radius, radius), (0, 0)))
    summed = jnp.zeros(surface.shape, F32)
    for offset in range(taps_count):
        summed = (
            summed
            + coefficients[offset].astype(F32)[:, :, None] * padded[:, offset : offset + columns, :]
        )
    return summed


def col_stencil(surface, coefficients):
    taps_count = coefficients.shape[0]
    radius = taps_count // 2
    lines = surface.shape[0]
    swapped = jnp.swapaxes(coefficients, 1, 2)
    padded = jnp.pad(surface.astype(F32), ((radius, radius), (0, 0), (0, 0)))
    summed = jnp.zeros(surface.shape, F32)
    for offset in range(taps_count):
        summed = (
            summed
            + swapped[offset].astype(F32)[:, :, None] * padded[offset : offset + lines, :, :]
        )
    return summed


def apply_layer(current, params):
    row_part = row_stencil(current, params[0]).astype(BF16)
    columns_view = lax.all_to_all(row_part, "space", split_axis=1, concat_axis=0, tiled=True)
    mixed_field = col_stencil(columns_view, params[1])
    inverse = lax.rsqrt(jnp.mean(mixed_field * mixed_field, axis=-1, keepdims=True) + 1e-06)
    normed = (mixed_field * inverse * params[2].astype(F32)).astype(BF16)
    hidden = jax.nn.gelu(
        jnp.dot(normed, params[3], preferred_element_type=F32) + params[4].astype(F32),
        approximate=True,
    ).astype(BF16)
    return (mixed_field + jnp.dot(hidden, params[5], preferred_element_type=F32)).astype(BF16)


def to_rows(output):
    return lax.all_to_all(output, "space", split_axis=0, concat_axis=1, tiled=True)


def read_density(output, readout):
    return jax.nn.softplus(jnp.dot(output, readout, preferred_element_type=F32))


def layers_over_sections(
    raster, row_coef, col_coef, norm_gain, weight_in, bias_in, weight_out, readout
):
    sections = lax.axis_size("section")
    spaces = lax.axis_size("space")
    windows = raster.shape[0]
    position = lax.axis_index("section")
    params = (row_coef[0], col_coef[0], norm_gain[0], weight_in[0], bias_in[0], weight_out[0])
    carried = jnp.zeros(raster.shape[1:], BF16)
    finished = jnp.zeros((windows, raster.shape[1] * spaces, raster.shape[2] // spaces), F32)
    for moment in range(windows + sections - 1):
        entering = raster[min(moment, windows - 1)]
        current = jnp.where(position == 0, entering, carried)
        output = apply_layer(current, params)
        finished_index = moment - (sections - 1)
        if finished_index >= 0:
            finished = finished.at[finished_index].set(read_density(output, readout))
        if moment < windows + sections - 2:
            carried = from_behind(to_rows(output), "section", 1)
    row_density = lax.all_to_all(finished, "space", split_axis=1, concat_axis=2, tiled=True)
    everyone = from_root(row_density, "section", sections - 1)
    return lax.dynamic_slice_in_dim(everyone, position, 1, 0)


TAPS = 15
RADIUS = 7
ROWS = 32
COLS = 16
WIDE = 128
CELLS = ROWS * COLS
GROUP = 8 * COLS


def call(kernel, outs, specs, scratch=(), room=48, place=VMEM):
    return pl.pallas_call(
        kernel,
        out_shape=outs,
        in_specs=specs,
        out_specs=jax.tree.map(lambda _: place, outs),
        scratch_shapes=list(scratch),
        compiler_params=pltpu.CompilerParams(vmem_limit_bytes=room * 1024 * 1024),
        cost_estimate=pl.CostEstimate(flops=1, bytes_accessed=1, transcendentals=0),
    )


def after(array, *others):
    return lax.optimization_barrier((array, *others))[0]


def shaped(shape, kind=BF16):
    return jax.ShapeDtypeStruct(shape, kind)


def iota(shape, axis):
    return lax.broadcasted_iota(jnp.int32, shape, axis)


def picked(which, values):
    out = values[0]
    for k in range(1, len(values)):
        out = jnp.where(which == k, values[k], out)
    return out


def position():
    s, p = lax.axis_index("section"), lax.axis_index("space")
    return s, p % 2, p // 2, p


def pack_kernel(weight_in, weight_out, bias, gain, out, half, biases, gains, arrive, leave):
    _, c, _, _ = position()
    start = pl.multiple_of(c * 256, 256)
    copies = [
        pltpu.make_async_copy(bias, biases, arrive.at[0]),
        pltpu.make_async_copy(gain, gains, arrive.at[1]),
        pltpu.make_async_copy(weight_in.at[0, :, pl.ds(start, 256)], half.at[0:256, :], arrive.at[2]),
        pltpu.make_async_copy(weight_out.at[0, pl.ds(start, 256), :], half.at[256:512, :], arrive.at[3]),
    ]
    for copy in copies:
        copy.start()
    for copy in copies[:2]:
        copy.wait()
    line = iota((16, 256), 0)
    part = jnp.where(c == 0, biases[:, 0:256].astype(F32), biases[:, 256:512].astype(F32))
    tail = jnp.where(line == 0, part, jnp.where(line == 1, gains[...].astype(F32), 0.0))
    half[512:528, :] = tail.astype(BF16)
    for copy in copies[2:]:
        copy.wait()
    copies = [pltpu.make_async_copy(half, out.at[n], leave.at[n]) for n in range(4)]
    for copy in copies:
        copy.start()
    for copy in copies:
        copy.wait()


def chunk_kernel(own_taps, sib_taps, own, sib, o0, o1, o2, o3, chunk):
    _, c, z, _ = position()
    channels = own.shape[-1]
    for i in range(8):
        cells = jnp.where(c == i // 4, own[i % 4], sib[i % 4]).reshape(4, 2, COLS, channels)
        chunk[:, COLS * i : COLS * (i + 1), :] = jnp.where(c == 0, cells[:, 0], cells[:, 1])
    first, second = own_taps[0:4].astype(F32), sib_taps[0:4].astype(F32)
    taps = jnp.concatenate([jnp.where(c == 0, first, second), jnp.where(c == 0, second, first)], 0)
    turned = jnp.transpose(taps.reshape(WIDE, WIDE)).reshape(16, 8, WIDE)
    for to in range(4):
        at = [jnp.where(c == 0, turned[(4 * to + d) % 16], turned[(4 * to + d + 2) % 16]) for d in (-1, 0, 1, 2)]
        sides = [jnp.concatenate([at[1], at[2]], 0), jnp.concatenate([at[0], at[3]], 0)]
        chunk[to, GROUP : GROUP + 16, :] = jnp.concatenate(sides, 1).astype(BF16)
        edge = [jnp.where(c == 0, sib_taps[m + 6], sib_taps[m + 4]) for m in range(2)]
        chunk[to, GROUP + 16 : GROUP + 32, :] = jnp.concatenate(edge, 1)
    for k, out in enumerate((o0, o1, o2, o3)):
        out[...] = chunk[z ^ k]


def assemble_kernel(g0, g1, g2, g3, own_taps, sib_taps, field, taps, edges):
    _, c, z, _ = position()
    for k, g in enumerate((g0, g1, g2, g3)):
        field[pl.ds(pl.multiple_of((z ^ k) * GROUP, GROUP), GROUP), :] = g[0:GROUP, :]
        taps[16 * k : 16 * (k + 1), :] = g[GROUP : GROUP + 16, :]
        edges[z ^ k] = g[GROUP + 16 : GROUP + 32, :]
    edge = edges[(z + 3 + 2 * c) % 4]
    for m in range(4):
        core, chip = sib_taps[4 + (m + 2) % 4], edge[:, WIDE * (m % 2) : WIDE * (m % 2 + 1)]
        margin = jnp.where(c == 0, chip, core) if m < 2 else jnp.where(c == 0, core, chip)
        taps[64 + 16 * m : 80 + 16 * m, 0:WIDE] = own_taps[4 + m]
        taps[64 + 16 * m : 80 + 16 * m, WIDE : 2 * WIDE] = margin


def prepare_kernel(layers, last, q0, q1, q2, q3, *rest):
    s, c, z, p = position()
    outs, (turned, ordered, parts) = list(rest[:-3]), rest[-3:]

    tap_in, tap_out = iota((WIDE, 256), 0), iota((WIDE, 256), 1)
    expand = jnp.where((tap_in == tap_out // COLS) & (tap_in < TAPS), 1.0, 0.0).astype(BF16)
    lane, line = iota((COLS, 256), 1), iota((COLS, 256), 0)
    same = line == lane % COLS

    def columns(table, out):
        for m in range(4):
            turned[128 * m : 128 * (m + 1), :] = jnp.concatenate(
                [jnp.transpose(table[16 * m : 16 * (m + 1)]), jnp.zeros((128, WIDE - 16), F32)], 1
            )
        for i in range(ROWS):
            ordered[COLS * i : COLS * (i + 1), :] = turned[pl.ds(i, COLS, stride=ROWS), :]
        wide = jnp.dot(ordered[...].astype(BF16), expand, preferred_element_type=F32)
        for i in range(ROWS):
            row = i + lane // COLS - RADIUS
            block = jnp.where(same & (row >= 0) & (row < ROWS), wide[COLS * i : COLS * (i + 1)], 0.0)
            block = jnp.concatenate([block, jnp.zeros((COLS, CELLS - 256), F32)], 1)
            shift = (COLS * (i - RADIUS)) % CELLS
            if shift:
                block = pltpu.roll(block, shift, 1)
            out[COLS * i : COLS * (i + 1), :] = block.astype(BF16)

    lane2, line2 = iota((GROUP, WIDE), 1), iota((GROUP, WIDE), 0)
    tap = (lane2 - line2 + RADIUS + WIDE) % WIDE
    source = line2 % COLS + tap - RADIUS
    inside = (tap < TAPS) & (source >= 0) & (source < COLS)
    on_left = (tap < TAPS) & (source < 0) & (p > 0)
    on_right = (tap < TAPS) & (source >= COLS) & (p < last)
    h = line2 % COLS
    tap_u = (lane2 - line2 - 1 + WIDE) % WIDE
    tap_v = (lane2 - line2 + 15 + WIDE) % WIDE
    u_left = (h < 8) & (tap_u < TAPS) & (h + tap_u < 15)
    u_own = (h >= 8) & (tap_u < TAPS) & (h + tap_u < 15)
    v_own = (h < 8) & (tap_v < TAPS) & (h + tap_v >= 15)
    v_right = (h >= 8) & (tap_v < TAPS) & (h + tap_v >= 15)

    def rolled(part, shift):
        return jnp.concatenate([pltpu.roll(part, shift, 1, stride=1, stride_axis=0)] * 8, 0)

    def sides(left, right):
        return jnp.where(c == 0, right, left).astype(BF16), jnp.where(c == 0, left, right).astype(BF16)

    for layer in layers:
        table = picked(s ^ layer, [q[...].astype(F32) for q in (q0, q1, q2, q3)])
        columns(table[64:128, 0:WIDE], outs.pop(0))
        if layer % 2 == 0:
            columns(table[64:128, WIDE : 2 * WIDE], outs.pop(0))
        out = outs.pop(0)
        for k in range(4):
            parts[z ^ k] = table[16 * k : 16 * (k + 1)]
        for g in range(4):
            part = parts[g]
            band = rolled(part[:, 0:WIDE], WIDE - RADIUS)
            left, right = jnp.where(on_left, band, 0.0), jnp.where(on_right, band, 0.0)
            out[g, 0:GROUP, 0:WIDE] = jnp.where(inside, band, 0.0).astype(BF16)
            if layer % 2 == 1:
                margin = pltpu.roll(left, 8, 1) + pltpu.roll(right, WIDE - 8, 1)
                out[g, 0:GROUP, WIDE : 2 * WIDE] = margin.astype(BF16)
                continue
            core, chip = sides(pltpu.roll(left, 16, 1), pltpu.roll(right, WIDE - 16, 1))
            out[g, 0:GROUP, WIDE : 2 * WIDE] = core
            out[g, 0:GROUP, 2 * WIDE : 3 * WIDE] = chip
            band = rolled(part[:, WIDE : 2 * WIDE], 1)
            back = pltpu.roll(band, WIDE - 16, 1)
            mid = jnp.where(u_own, band, jnp.where(v_own, back, 0.0))
            core, chip = sides(jnp.where(u_left, band, 0.0), jnp.where(v_right, back, 0.0))
            out[g, GROUP : 2 * GROUP, 0:WIDE] = mid.astype(BF16)
            out[g, GROUP : 2 * GROUP, WIDE : 2 * WIDE] = core
            out[g, GROUP : 2 * GROUP, 2 * WIDE : 3 * WIDE] = chip


def layer_kernel(layer, fields, final, *refs):
    cells, refs = refs[:fields], refs[fields:]
    wide = fields == 3
    bands, refs = refs[0], refs[1:]
    col_bands, refs = refs[: 1 + wide], refs[1 + wide :]
    if final:
        readout, refs = refs[0], refs[1:]
    mine, theirs, refs = refs[0], refs[1], refs[2:]
    outs, (weights, sems) = refs[: 1 + wide], refs[1 + wide : 3 + wide]
    rows = refs[3 + wide :]
    copies = [
        pltpu.make_async_copy(half, weights.at[n], sems.at[n])
        for n, half in enumerate((mine.at[layer], theirs.at[max(layer - 1, 0)]))
    ]
    for copy in copies:
        copy.start()
    channels = cells[0].shape[-1]
    for g in range(4):
        cut = slice(GROUP * g, GROUP * (g + 1))
        stacked = jnp.concatenate([x[cut] for x in cells], 0)
        done = jnp.dot(bands[g], stacked, preferred_element_type=F32).astype(BF16)
        for n, row in enumerate(rows):
            row[cut, :] = done[GROUP * n : GROUP * (n + 1)]
    size = 256
    mixed = [
        jnp.dot(band[size * b : size * (b + 1), :], row[...], preferred_element_type=F32)
        for band, row in zip(col_bands, rows)
        for b in range(CELLS // size)
    ]
    for copy in copies:
        copy.wait()
    gain = weights[0, 512:528, :].astype(F32)[1:2]
    for n, total in enumerate(mixed):
        inverse = lax.rsqrt(jnp.mean(total * total, axis=-1, keepdims=True) + 1e-06)
        normed = (total * inverse * gain).astype(BF16)
        parts = []
        for half in range(2):
            bias = weights[half, 512:528, :].astype(F32)[0:1]
            hidden = jnp.dot(normed, weights[half, 0:256, :], preferred_element_type=F32) + bias
            hidden = jax.nn.gelu(hidden, approximate=True).astype(BF16)
            parts.append(jnp.dot(hidden, weights[half, 256:512, :], preferred_element_type=F32))
        total = (total + (parts[0] + parts[1])).astype(BF16)
        out, b = outs[n // 2], n % 2
        if final:
            reader = jnp.broadcast_to(readout[...], (8, channels))
            logit = lax.dot_general(reader, total, (((1,), (1,)), ((), ())), preferred_element_type=F32)
            logit = jnp.maximum(logit, 0.0) + jnp.log1p(jnp.exp(-jnp.abs(logit)))
            for d in range(4):
                moved = pltpu.roll(logit, size - 64 * d, 1) if d else logit
                out[4 * b + d : 4 * b + d + 1, :] = moved[0:1, 0:WIDE]
        else:
            out[size * b : size * (b + 1), :] = total


def gather_kernel(got, out):
    lane, line = iota((8, WIDE), 1), iota((8, WIDE), 0)
    mask = lane // COLS == line
    cells = pltpu.roll(got[...], 0, 1, stride=COLS, stride_axis=0)
    for t in range(4):
        moved = pltpu.roll(cells, WIDE - COLS * t, 1) if t else cells
        out[0, t : t + 1, :] = jnp.sum(jnp.where(mask, moved, 0.0), axis=0, keepdims=True)


def window_on_section(raster, row_coef, col_coef, norm_gain, weight_in, bias_in, weight_out, readout):
    c = lax.axis_index("space") % 2
    channels = raster.shape[-1]
    spaces = lax.axis_size("space")

    def core(array):
        return lax.ppermute(array, "space", [(i, i ^ 1) for i in range(spaces)])

    def chip(array, k):
        return lax.ppermute(array, "space", [(i, i ^ (2 * k)) for i in range(spaces)])

    def section(array, k):
        return lax.ppermute(array, "section", [(i, i ^ k) for i in range(4)])

    def beside(array):
        pairs = []
        for a in range(4):
            for q in range(spaces):
                other = q - 1 if q % 2 == 0 else q + 1
                to = a * spaces + other if 0 <= other < spaces else (a ^ 1) * spaces + q
                pairs.append((a * spaces + q, to))
        return lax.ppermute(array, ("section", "space"), pairs)

    window = lax.dynamic_index_in_dim(raster, lax.axis_index("section"), 0, keepdims=False)
    window_sib = core(window)
    packed = call(
        pack_kernel,
        shaped((4, 528, 256)),
        [ANY] * 4,
        [
            pltpu.VMEM((528, 256), BF16),
            pltpu.VMEM((1, 512), BF16),
            pltpu.VMEM((1, 256), BF16),
            pltpu.SemaphoreType.DMA((4,)),
            pltpu.SemaphoreType.DMA((4,)),
        ],
        room=60,
        place=ANY,
    )(weight_in, weight_out, bias_in, norm_gain)
    own = jnp.concatenate([row_coef[0], col_coef[0].reshape(TAPS, 4, WIDE)], 1)
    own = jnp.pad(jnp.swapaxes(own, 0, 1), ((0, 0), (0, 1), (0, 0)))
    sib = core(own)

    chunks = call(
        chunk_kernel,
        (shaped((GROUP + 32, channels)),) * 4,
        [VMEM] * 4,
        [pltpu.VMEM((4, GROUP + 32, channels), BF16)],
    )(own, sib, window, window_sib)
    sent = chunks
    chunks = [sent[0]] + [chip(sent[k], k) for k in (1, 2, 3)]

    packed = after(packed, window_sib, sib)
    mine = lax.all_to_all(packed, "section", split_axis=0, concat_axis=0, tiled=True)

    field, taps = call(
        assemble_kernel,
        (shaped((CELLS, channels)), shaped((WIDE, 256))),
        [VMEM] * 6,
        [pltpu.VMEM((4, 16, 256), BF16)],
    )(*chunks, own, sib)
    field_core, field_chip = core(field), beside(field)
    tables = [taps] + [section(taps, k) for k in (1, 2, 3)]
    theirs = [core(after(mine[:1], field_chip, *tables)), core(after(mine[1:], field_chip, *tables))]

    def prepare(layers, tables):
        outs = []
        for layer in layers:
            even = layer % 2 == 0
            outs += [shaped((CELLS, CELLS))] * (1 + even)
            outs.append(shaped((4, 2 * GROUP, 3 * WIDE) if even else (4, GROUP, 2 * WIDE)))
        return call(
            functools.partial(prepare_kernel, layers, spaces - 1),
            tuple(outs),
            [VMEM] * 4,
            [pltpu.VMEM((CELLS, WIDE), F32), pltpu.VMEM((CELLS, WIDE), F32), pltpu.VMEM((4, 16, 256), F32)],
        )(*tables)

    def run(layer, cells, bands, readers=()):
        wide = len(cells) == 3
        final = bool(readers)
        outs = (shaped((8, WIDE), F32),) if final else (shaped((CELLS, channels)),) * (1 + wide)
        return call(
            functools.partial(layer_kernel, layer, len(cells), final),
            outs,
            [VMEM] * (len(cells) + 2 + wide + final) + [ANY] * 2,
            [pltpu.VMEM((2, 528, 256), BF16), pltpu.SemaphoreType.DMA((2,))]
            + [pltpu.VMEM((CELLS, channels), BF16)] * (1 + wide),
        )(*cells, bands[-1], *bands[:-1], *readers, mine, theirs[layer > 0])

    bands0 = prepare((0,), [after(tables[0], field_chip)] + tables[1:])
    cells = run(0, (field, field_core, field_chip), bands0)
    bands1 = prepare((1,), [after(tables[0], cells[0])] + tables[1:])
    (state,) = run(1, cells, bands1)
    bands23 = prepare((2, 3), [after(t, state) for t in tables])
    cells = run(2, (state, core(state), beside(state)), bands23[:3])
    (density,) = run(3, cells, bands23[3:], (readout.reshape(1, channels),))

    density = lax.all_to_all(density, "space", split_axis=0, concat_axis=0, tiled=True)
    return call(gather_kernel, shaped((1, 4, WIDE), F32), [VMEM])(density)


def on_device(raster, row_coef, *rest):
    fits = (
        lax.axis_size("section") == 4
        and lax.axis_size("space") == 8
        and raster.shape == (4, 4, WIDE, 256)
        and row_coef.shape[1] == TAPS
    )
    plan = window_on_section if fits else layers_over_sections
    return plan(raster, row_coef, *rest)


def solution(mesh):
    placed = (
        P(None, "space", None, None),
        P("section", None, "space", None),
        P("section", None, "space", None),
        P("section", None),
        P("section", None, None),
        P("section", None),
        P("section", None, None),
        P(),
    )
    return jax.shard_map(
        on_device,
        mesh=mesh,
        in_specs=placed,
        out_specs=P("section", "space", None),
        check_vma=False,
    )
```

```python
import functools

import jax
import jax.numpy as jnp
from jax import lax
from jax.experimental import pallas as pl
from jax.experimental.pallas import tpu as pltpu
from jax.sharding import PartitionSpec as P

F32 = jnp.float32
BF16 = jnp.bfloat16
VMEM = pl.BlockSpec(memory_space=pltpu.VMEM)
ANY = pl.BlockSpec(memory_space=pl.ANY)


def from_behind(array, axis, by):
    size = lax.axis_size(axis)
    pairs = [(i, i + by) for i in range(size) if 0 <= i + by < size]
    return lax.ppermute(array, axis, pairs)


def from_root(value, axis, source):
    kept = jnp.where(lax.axis_index(axis) == source, value, 0).astype(value.dtype)
    return lax.psum(kept, axis)


def row_stencil(surface, coefficients):
    taps_count = coefficients.shape[0]
    radius = taps_count // 2
    columns = surface.shape[1]
    padded = jnp.pad(surface.astype(F32), ((0, 0), (radius, radius), (0, 0)))
    summed = jnp.zeros(surface.shape, F32)
    for offset in range(taps_count):
        summed = (
            summed
            + coefficients[offset].astype(F32)[:, :, None] * padded[:, offset : offset + columns, :]
        )
    return summed


def col_stencil(surface, coefficients):
    taps_count = coefficients.shape[0]
    radius = taps_count // 2
    lines = surface.shape[0]
    swapped = jnp.swapaxes(coefficients, 1, 2)
    padded = jnp.pad(surface.astype(F32), ((radius, radius), (0, 0), (0, 0)))
    summed = jnp.zeros(surface.shape, F32)
    for offset in range(taps_count):
        summed = (
            summed
            + swapped[offset].astype(F32)[:, :, None] * padded[offset : offset + lines, :, :]
        )
    return summed


def apply_layer(current, params):
    row_part = row_stencil(current, params[0]).astype(BF16)
    columns_view = lax.all_to_all(row_part, "space", split_axis=1, concat_axis=0, tiled=True)
    mixed_field = col_stencil(columns_view, params[1])
    inverse = lax.rsqrt(jnp.mean(mixed_field * mixed_field, axis=-1, keepdims=True) + 1e-06)
    normed = (mixed_field * inverse * params[2].astype(F32)).astype(BF16)
    hidden = jax.nn.gelu(
        jnp.dot(normed, params[3], preferred_element_type=F32) + params[4].astype(F32),
        approximate=True,
    ).astype(BF16)
    return (mixed_field + jnp.dot(hidden, params[5], preferred_element_type=F32)).astype(BF16)


def to_rows(output):
    return lax.all_to_all(output, "space", split_axis=0, concat_axis=1, tiled=True)


def read_density(output, readout):
    return jax.nn.softplus(jnp.dot(output, readout, preferred_element_type=F32))


def layers_over_sections(
    raster, row_coef, col_coef, norm_gain, weight_in, bias_in, weight_out, readout
):
    sections = lax.axis_size("section")
    spaces = lax.axis_size("space")
    windows = raster.shape[0]
    position = lax.axis_index("section")
    params = (row_coef[0], col_coef[0], norm_gain[0], weight_in[0], bias_in[0], weight_out[0])
    carried = jnp.zeros(raster.shape[1:], BF16)
    finished = jnp.zeros((windows, raster.shape[1] * spaces, raster.shape[2] // spaces), F32)
    for moment in range(windows + sections - 1):
        entering = raster[min(moment, windows - 1)]
        current = jnp.where(position == 0, entering, carried)
        output = apply_layer(current, params)
        finished_index = moment - (sections - 1)
        if finished_index >= 0:
            finished = finished.at[finished_index].set(read_density(output, readout))
        if moment < windows + sections - 2:
            carried = from_behind(to_rows(output), "section", 1)
    row_density = lax.all_to_all(finished, "space", split_axis=1, concat_axis=2, tiled=True)
    everyone = from_root(row_density, "section", sections - 1)
    return lax.dynamic_slice_in_dim(everyone, position, 1, 0)


TAPS = 15
RADIUS = 7
ROWS = 32
COLS = 16
WIDE = 128
CELLS = ROWS * COLS
GROUP = 8 * COLS


def call(kernel, outs, specs, scratch=(), room=48, place=VMEM):
    return pl.pallas_call(
        kernel,
        out_shape=outs,
        in_specs=specs,
        out_specs=jax.tree.map(lambda _: place, outs),
        scratch_shapes=list(scratch),
        compiler_params=pltpu.CompilerParams(vmem_limit_bytes=room * 1024 * 1024),
        cost_estimate=pl.CostEstimate(flops=1, bytes_accessed=1, transcendentals=0),
    )


def after(array, *others):
    return lax.optimization_barrier((array, *others))[0]


def shaped(shape, kind=BF16):
    return jax.ShapeDtypeStruct(shape, kind)


def iota(shape, axis):
    return lax.broadcasted_iota(jnp.int32, shape, axis)


def picked(which, values):
    out = values[0]
    for k in range(1, len(values)):
        out = jnp.where(which == k, values[k], out)
    return out


def position():
    s, p = lax.axis_index("section"), lax.axis_index("space")
    return s, p % 2, p // 2, p


def stage_kernel(row_coef, col_coef, weight_in, weight_out, bias, gain, out, own, *scratch):
    rows, cols, biases, gains, half, taps, arrive, leave = scratch
    _, c, _, _ = position()
    start = pl.multiple_of(c * 256, 256)
    copies = [
        pltpu.make_async_copy(row_coef.at[0], rows, arrive.at[0]),
        pltpu.make_async_copy(col_coef.at[0], cols, arrive.at[1]),
        pltpu.make_async_copy(bias, biases, arrive.at[2]),
        pltpu.make_async_copy(gain, gains, arrive.at[3]),
        pltpu.make_async_copy(weight_in.at[0, :, pl.ds(start, 256)], half.at[0:256, :], arrive.at[4]),
        pltpu.make_async_copy(weight_out.at[0, pl.ds(start, 256), :], half.at[256:512, :], arrive.at[5]),
    ]
    for copy in copies:
        copy.start()
    for copy in copies[2:4]:
        copy.wait()
    line = iota((16, 256), 0)
    part = jnp.where(c == 0, biases[:, 0:256].astype(F32), biases[:, 256:512].astype(F32))
    tail = jnp.where(line == 0, part, jnp.where(line == 1, gains[...].astype(F32), 0.0))
    half[512:528, :] = tail.astype(BF16)
    for copy in copies[4:]:
        copy.wait()
    sends = [pltpu.make_async_copy(half, out.at[n], leave.at[n]) for n in range(4)]
    for copy in sends:
        copy.start()
    for copy in copies[:2]:
        copy.wait()
    zero = jnp.zeros((1, WIDE), F32)
    row, col = rows[...].astype(F32), cols[...].astype(F32)
    for m in range(4):
        taps[m] = jnp.concatenate([row[:, m, :], zero], 0).astype(BF16)
        group = jnp.concatenate([col[:, 4 * m + j, :] for j in range(4)], 1)
        taps[4 + m] = jnp.concatenate([group, zero], 0).astype(BF16)
    sends.append(pltpu.make_async_copy(taps, own, leave.at[4]))
    sends[-1].start()
    for copy in sends:
        copy.wait()


def chunk_kernel(own_taps, sib_taps, own, sib, o0, o1, o2, o3, chunk):
    _, c, z, _ = position()
    channels = own.shape[-1]
    for i in range(8):
        cells = jnp.where(c == i // 4, own[i % 4], sib[i % 4]).reshape(4, 2, COLS, channels)
        chunk[:, COLS * i : COLS * (i + 1), :] = jnp.where(c == 0, cells[:, 0], cells[:, 1])
    first, second = own_taps[0:4].astype(F32), sib_taps[0:4].astype(F32)
    taps = jnp.concatenate([jnp.where(c == 0, first, second), jnp.where(c == 0, second, first)], 0)
    turned = jnp.transpose(taps.reshape(WIDE, WIDE)).reshape(16, 8, WIDE)
    for to in range(4):
        at = [jnp.where(c == 0, turned[(4 * to + d) % 16], turned[(4 * to + d + 2) % 16]) for d in (-1, 0, 1, 2)]
        sides = [jnp.concatenate([at[1], at[2]], 0), jnp.concatenate([at[0], at[3]], 0)]
        chunk[to, GROUP : GROUP + 16, :] = jnp.concatenate(sides, 1).astype(BF16)
        edge = [jnp.where(c == 0, sib_taps[m + 6], sib_taps[m + 4]) for m in range(2)]
        chunk[to, GROUP + 16 : GROUP + 32, :] = jnp.concatenate(edge, 1)
    for k, out in enumerate((o0, o1, o2, o3)):
        out[...] = chunk[z ^ k]


def tables_kernel(g0, g3, g2, g1, own_taps, sib_taps, taps, edges):
    _, c, z, _ = position()
    for k, g in enumerate((g0, g1, g2, g3)):
        taps[16 * k : 16 * (k + 1), :] = g[GROUP : GROUP + 16, :]
        edges[z ^ k] = g[GROUP + 16 : GROUP + 32, :]
    edge = edges[(z + 3 + 2 * c) % 4]
    for m in range(4):
        core, chip = sib_taps[4 + (m + 2) % 4], edge[:, WIDE * (m % 2) : WIDE * (m % 2 + 1)]
        margin = jnp.where(c == 0, chip, core) if m < 2 else jnp.where(c == 0, core, chip)
        taps[64 + 16 * m : 80 + 16 * m, 0:WIDE] = own_taps[4 + m]
        taps[64 + 16 * m : 80 + 16 * m, WIDE : 2 * WIDE] = margin


def field_kernel(g0, g3, g2, g1, field):
    _, _, z, _ = position()
    for k, g in enumerate((g0, g1, g2, g3)):
        field[pl.ds(pl.multiple_of((z ^ k) * GROUP, GROUP), GROUP), :] = g[0:GROUP, :]


def prepare_kernel(layers, last, q0, q3, q2, q1, *rest):
    s, c, z, p = position()
    outs, (turned, ordered, parts) = list(rest[:-3]), rest[-3:]

    tap_in, tap_out = iota((WIDE, 256), 0), iota((WIDE, 256), 1)
    expand = jnp.where((tap_in == tap_out // COLS) & (tap_in < TAPS), 1.0, 0.0).astype(BF16)
    lane, line = iota((COLS, 256), 1), iota((COLS, 256), 0)
    same = line == lane % COLS

    def columns(table, out):
        for m in range(4):
            turned[128 * m : 128 * (m + 1), :] = jnp.concatenate(
                [jnp.transpose(table[16 * m : 16 * (m + 1)]), jnp.zeros((128, WIDE - 16), F32)], 1
            )
        for i in range(ROWS):
            ordered[COLS * i : COLS * (i + 1), :] = turned[pl.ds(i, COLS, stride=ROWS), :]
        wide = jnp.dot(ordered[...].astype(BF16), expand, preferred_element_type=F32)
        for i in range(ROWS):
            row = i + lane // COLS - RADIUS
            block = jnp.where(same & (row >= 0) & (row < ROWS), wide[COLS * i : COLS * (i + 1)], 0.0)
            block = jnp.concatenate([block, jnp.zeros((COLS, CELLS - 256), F32)], 1)
            shift = (COLS * (i - RADIUS)) % CELLS
            if shift:
                block = pltpu.roll(block, shift, 1)
            out[COLS * i : COLS * (i + 1), :] = block.astype(BF16)

    lane2, line2 = iota((GROUP, WIDE), 1), iota((GROUP, WIDE), 0)
    tap = (lane2 - line2 + RADIUS + WIDE) % WIDE
    source = line2 % COLS + tap - RADIUS
    inside = (tap < TAPS) & (source >= 0) & (source < COLS)
    on_left = (tap < TAPS) & (source < 0) & (p > 0)
    on_right = (tap < TAPS) & (source >= COLS) & (p < last)
    h = line2 % COLS
    tap_u = (lane2 - line2 - 1 + WIDE) % WIDE
    tap_v = (lane2 - line2 + 15 + WIDE) % WIDE
    u_left = (h < 8) & (tap_u < TAPS) & (h + tap_u < 15)
    u_own = (h >= 8) & (tap_u < TAPS) & (h + tap_u < 15)
    v_own = (h < 8) & (tap_v < TAPS) & (h + tap_v >= 15)
    v_right = (h >= 8) & (tap_v < TAPS) & (h + tap_v >= 15)

    def rolled(part, shift):
        return jnp.concatenate([pltpu.roll(part, shift, 1, stride=1, stride_axis=0)] * 8, 0)

    def sides(left, right):
        return jnp.where(c == 0, right, left).astype(BF16), jnp.where(c == 0, left, right).astype(BF16)

    for layer in layers:
        table = picked(s ^ layer, [q[...].astype(F32) for q in (q0, q1, q2, q3)])
        columns(table[64:128, 0:WIDE], outs.pop(0))
        if layer % 2 == 0:
            columns(table[64:128, WIDE : 2 * WIDE], outs.pop(0))
        out = outs.pop(0)
        for k in range(4):
            parts[z ^ k] = table[16 * k : 16 * (k + 1)]
        for g in range(4):
            part = parts[g]
            band = rolled(part[:, 0:WIDE], WIDE - RADIUS)
            left, right = jnp.where(on_left, band, 0.0), jnp.where(on_right, band, 0.0)
            out[g, 0:GROUP, 0:WIDE] = jnp.where(inside, band, 0.0).astype(BF16)
            if layer % 2 == 1:
                margin = pltpu.roll(left, 8, 1) + pltpu.roll(right, WIDE - 8, 1)
                out[g, 0:GROUP, WIDE : 2 * WIDE] = margin.astype(BF16)
                continue
            core, chip = sides(pltpu.roll(left, 16, 1), pltpu.roll(right, WIDE - 16, 1))
            out[g, 0:GROUP, WIDE : 2 * WIDE] = core
            out[g, 0:GROUP, 2 * WIDE : 3 * WIDE] = chip
            band = rolled(part[:, WIDE : 2 * WIDE], 1)
            back = pltpu.roll(band, WIDE - 16, 1)
            mid = jnp.where(u_own, band, jnp.where(v_own, back, 0.0))
            core, chip = sides(jnp.where(u_left, band, 0.0), jnp.where(v_right, back, 0.0))
            out[g, GROUP : 2 * GROUP, 0:WIDE] = mid.astype(BF16)
            out[g, GROUP : 2 * GROUP, WIDE : 2 * WIDE] = core
            out[g, GROUP : 2 * GROUP, 2 * WIDE : 3 * WIDE] = chip


def layer_kernel(layer, fields, final, *refs):
    cells, refs = refs[:fields], refs[fields:]
    wide = fields == 3
    bands, refs = refs[0], refs[1:]
    col_bands, refs = refs[: 1 + wide], refs[1 + wide :]
    if final:
        readout, refs = refs[0], refs[1:]
    mine, theirs, refs = refs[0], refs[1], refs[2:]
    outs, rows = refs[: 1 + wide], refs[1 + wide :]
    halves = (mine.at[layer], theirs.at[max(layer - 1, 0)])
    channels = cells[0].shape[-1]
    for g in range(4):
        cut = slice(GROUP * g, GROUP * (g + 1))
        stacked = jnp.concatenate([x[cut] for x in cells], 0)
        done = jnp.dot(bands[g], stacked, preferred_element_type=F32).astype(BF16)
        for n, row in enumerate(rows):
            row[cut, :] = done[GROUP * n : GROUP * (n + 1)]
    size = 256
    mixed = [
        jnp.dot(band[size * b : size * (b + 1), :], row[...], preferred_element_type=F32)
        for band, row in zip(col_bands, rows)
        for b in range(CELLS // size)
    ]
    gain = halves[0][512:528, :].astype(F32)[1:2]
    for n, total in enumerate(mixed):
        inverse = lax.rsqrt(jnp.mean(total * total, axis=-1, keepdims=True) + 1e-06)
        normed = (total * inverse * gain).astype(BF16)
        parts = []
        for half in halves:
            bias = half[512:528, :].astype(F32)[0:1]
            hidden = jnp.dot(normed, half[0:256, :], preferred_element_type=F32) + bias
            hidden = jax.nn.gelu(hidden, approximate=True).astype(BF16)
            parts.append(jnp.dot(hidden, half[256:512, :], preferred_element_type=F32))
        total = (total + (parts[0] + parts[1])).astype(BF16)
        out, b = outs[n // 2], n % 2
        if final:
            reader = jnp.broadcast_to(readout[...], (8, channels))
            logit = lax.dot_general(reader, total, (((1,), (1,)), ((), ())), preferred_element_type=F32)
            logit = jnp.maximum(logit, 0.0) + jnp.log1p(jnp.exp(-jnp.abs(logit)))
            for d in range(4):
                moved = pltpu.roll(logit, size - 64 * d, 1) if d else logit
                out[4 * b + d : 4 * b + d + 1, :] = moved[0:1, 0:WIDE]
        else:
            out[size * b : size * (b + 1), :] = total


def gather_kernel(got, out):
    lane, line = iota((8, WIDE), 1), iota((8, WIDE), 0)
    mask = lane // COLS == line
    cells = pltpu.roll(got[...], 0, 1, stride=COLS, stride_axis=0)
    for t in range(4):
        moved = pltpu.roll(cells, WIDE - COLS * t, 1) if t else cells
        out[0, t : t + 1, :] = jnp.sum(jnp.where(mask, moved, 0.0), axis=0, keepdims=True)


def window_on_section(raster, row_coef, col_coef, norm_gain, weight_in, bias_in, weight_out, readout):
    c = lax.axis_index("space") % 2
    channels = raster.shape[-1]
    spaces = lax.axis_size("space")

    def core(array):
        return lax.ppermute(array, "space", [(i, i ^ 1) for i in range(spaces)])

    def chip(array, k):
        return lax.ppermute(array, "space", [(i, i ^ (2 * k)) for i in range(spaces)])

    def section(array, k):
        return lax.ppermute(array, "section", [(i, i ^ k) for i in range(4)])

    def beside(array, ends=True):
        pairs = []
        for a in range(4):
            for q in range(spaces):
                other = q - 1 if q % 2 == 0 else q + 1
                to = a * spaces + other if 0 <= other < spaces else (a ^ 1) * spaces + q
                if ends or 0 <= other < spaces:
                    pairs.append((a * spaces + q, to))
        return lax.ppermute(array, ("section", "space"), pairs)

    window = lax.dynamic_index_in_dim(raster, lax.axis_index("section"), 0, keepdims=False)
    window_sib = core(window)
    packed, own = call(
        stage_kernel,
        (shaped((4, 528, 256)), shaped((8, 16, WIDE))),
        [ANY] * 6,
        [
            pltpu.VMEM(row_coef.shape[1:], BF16),
            pltpu.VMEM(col_coef.shape[1:], BF16),
            pltpu.VMEM((1, 512), BF16),
            pltpu.VMEM((1, 256), BF16),
            pltpu.VMEM((528, 256), BF16),
            pltpu.VMEM((8, 16, WIDE), BF16),
            pltpu.SemaphoreType.DMA((6,)),
            pltpu.SemaphoreType.DMA((5,)),
        ],
        room=60,
        place=ANY,
    )(row_coef, col_coef, weight_in, weight_out, bias_in, norm_gain)
    sib = core(own)

    chunks = call(
        chunk_kernel,
        (shaped((GROUP + 32, channels)),) * 4,
        [VMEM] * 4,
        [pltpu.VMEM((4, GROUP + 32, channels), BF16)],
    )(own, sib, window, window_sib)
    sent = chunks
    chunks = [sent[0]] + [chip(sent[k], k) for k in (3, 2, 1)][::-1]

    mine = lax.all_to_all(packed, "section", split_axis=0, concat_axis=0, tiled=True)

    taps = call(
        tables_kernel, shaped((WIDE, 256)), [VMEM] * 6, [pltpu.VMEM((4, 16, 256), BF16)]
    )(chunks[0], *chunks[:0:-1], own, sib)
    field = call(field_kernel, shaped((CELLS, channels)), [VMEM] * 4)(after(chunks[0], taps), *chunks[:0:-1])
    field_core, field_chip = core(field), beside(field)
    tables = [section(taps, k) for k in (3, 2, 1)]
    tables = [taps] + tables[::-1]
    theirs = [core(after(m, *tables[::-1], field_core, field_chip)) for m in (mine[:1], mine[1:])]

    def prepare(layers, tables):
        outs = []
        for layer in layers:
            even = layer % 2 == 0
            outs += [shaped((CELLS, CELLS))] * (1 + even)
            outs.append(shaped((4, 2 * GROUP, 3 * WIDE) if even else (4, GROUP, 2 * WIDE)))
        return call(
            functools.partial(prepare_kernel, layers, spaces - 1),
            tuple(outs),
            [VMEM] * 4,
            [pltpu.VMEM((CELLS, WIDE), F32), pltpu.VMEM((CELLS, WIDE), F32), pltpu.VMEM((4, 16, 256), F32)],
        )(tables[0], *tables[:0:-1])

    def run(layer, cells, bands, readers=()):
        wide = len(cells) == 3
        final = bool(readers)
        outs = (shaped((8, WIDE), F32),) if final else (shaped((CELLS, channels)),) * (1 + wide)
        return call(
            functools.partial(layer_kernel, layer, len(cells), final),
            outs,
            [VMEM] * (len(cells) + 4 + wide + final),
            [pltpu.VMEM((CELLS, channels), BF16)] * (1 + wide),
        )(*cells, bands[-1], *bands[:-1], *readers, mine, theirs[layer > 0])

    bands0 = prepare((0,), [after(tables[0], field_chip)] + tables[1:])
    cells = run(0, (field, field_core, field_chip), bands0)
    bands1 = prepare((1,), [after(tables[0], field_chip)] + tables[1:])
    (state,) = run(1, cells, bands1)
    bands23 = prepare((2, 3), [after(t, state) for t in tables])
    cells = run(2, (state, core(state), beside(state)), bands23[:3])
    (density,) = run(3, cells, bands23[3:], (readout.reshape(1, channels),))

    density = lax.all_to_all(density, "space", split_axis=0, concat_axis=0, tiled=True)
    return call(gather_kernel, shaped((1, 4, WIDE), F32), [VMEM])(density)


def on_device(raster, row_coef, *rest):
    fits = (
        lax.axis_size("section") == 4
        and lax.axis_size("space") == 8
        and raster.shape == (4, 4, WIDE, 256)
        and row_coef.shape[1] == TAPS
    )
    plan = window_on_section if fits else layers_over_sections
    return plan(raster, row_coef, *rest)


def solution(mesh):
    placed = (
        P(None, "space", None, None),
        P("section", None, "space", None),
        P("section", None, "space", None),
        P("section", None),
        P("section", None, None),
        P("section", None),
        P("section", None, None),
        P(),
    )
    return jax.shard_map(
        on_device,
        mesh=mesh,
        in_specs=placed,
        out_specs=P("section", "space", None),
        check_vma=False,
    )
```

```python
import functools

import jax
import jax.numpy as jnp
from jax import lax
from jax.experimental import pallas as pl
from jax.experimental.pallas import tpu as pltpu
from jax.sharding import PartitionSpec as P

F32 = jnp.float32
BF16 = jnp.bfloat16
VMEM = pl.BlockSpec(memory_space=pltpu.VMEM)
ANY = pl.BlockSpec(memory_space=pl.ANY)


def from_behind(array, axis, by):
    size = lax.axis_size(axis)
    pairs = [(i, i + by) for i in range(size) if 0 <= i + by < size]
    return lax.ppermute(array, axis, pairs)


def from_root(value, axis, source):
    kept = jnp.where(lax.axis_index(axis) == source, value, 0).astype(value.dtype)
    return lax.psum(kept, axis)


def row_stencil(surface, coefficients):
    taps_count = coefficients.shape[0]
    radius = taps_count // 2
    columns = surface.shape[1]
    padded = jnp.pad(surface.astype(F32), ((0, 0), (radius, radius), (0, 0)))
    summed = jnp.zeros(surface.shape, F32)
    for offset in range(taps_count):
        summed = (
            summed
            + coefficients[offset].astype(F32)[:, :, None] * padded[:, offset : offset + columns, :]
        )
    return summed


def col_stencil(surface, coefficients):
    taps_count = coefficients.shape[0]
    radius = taps_count // 2
    lines = surface.shape[0]
    swapped = jnp.swapaxes(coefficients, 1, 2)
    padded = jnp.pad(surface.astype(F32), ((radius, radius), (0, 0), (0, 0)))
    summed = jnp.zeros(surface.shape, F32)
    for offset in range(taps_count):
        summed = (
            summed
            + swapped[offset].astype(F32)[:, :, None] * padded[offset : offset + lines, :, :]
        )
    return summed


def apply_layer(current, params):
    row_part = row_stencil(current, params[0]).astype(BF16)
    columns_view = lax.all_to_all(row_part, "space", split_axis=1, concat_axis=0, tiled=True)
    mixed_field = col_stencil(columns_view, params[1])
    inverse = lax.rsqrt(jnp.mean(mixed_field * mixed_field, axis=-1, keepdims=True) + 1e-06)
    normed = (mixed_field * inverse * params[2].astype(F32)).astype(BF16)
    hidden = jax.nn.gelu(
        jnp.dot(normed, params[3], preferred_element_type=F32) + params[4].astype(F32),
        approximate=True,
    ).astype(BF16)
    return (mixed_field + jnp.dot(hidden, params[5], preferred_element_type=F32)).astype(BF16)


def to_rows(output):
    return lax.all_to_all(output, "space", split_axis=0, concat_axis=1, tiled=True)


def read_density(output, readout):
    return jax.nn.softplus(jnp.dot(output, readout, preferred_element_type=F32))


def layers_over_sections(
    raster, row_coef, col_coef, norm_gain, weight_in, bias_in, weight_out, readout
):
    sections = lax.axis_size("section")
    spaces = lax.axis_size("space")
    windows = raster.shape[0]
    position = lax.axis_index("section")
    params = (row_coef[0], col_coef[0], norm_gain[0], weight_in[0], bias_in[0], weight_out[0])
    carried = jnp.zeros(raster.shape[1:], BF16)
    finished = jnp.zeros((windows, raster.shape[1] * spaces, raster.shape[2] // spaces), F32)
    for moment in range(windows + sections - 1):
        entering = raster[min(moment, windows - 1)]
        current = jnp.where(position == 0, entering, carried)
        output = apply_layer(current, params)
        finished_index = moment - (sections - 1)
        if finished_index >= 0:
            finished = finished.at[finished_index].set(read_density(output, readout))
        if moment < windows + sections - 2:
            carried = from_behind(to_rows(output), "section", 1)
    row_density = lax.all_to_all(finished, "space", split_axis=1, concat_axis=2, tiled=True)
    everyone = from_root(row_density, "section", sections - 1)
    return lax.dynamic_slice_in_dim(everyone, position, 1, 0)


TAPS = 15
RADIUS = 7
ROWS = 32
COLS = 16
WIDE = 128
CELLS = ROWS * COLS
GROUP = 8 * COLS


def call(kernel, outs, specs, scratch=(), room=48, place=VMEM):
    return pl.pallas_call(
        kernel,
        out_shape=outs,
        in_specs=specs,
        out_specs=jax.tree.map(lambda _: place, outs),
        scratch_shapes=list(scratch),
        compiler_params=pltpu.CompilerParams(vmem_limit_bytes=room * 1024 * 1024),
        cost_estimate=pl.CostEstimate(flops=1, bytes_accessed=1, transcendentals=0),
    )


def after(array, *others):
    return lax.optimization_barrier((array, *others))[0]


def shaped(shape, kind=BF16):
    return jax.ShapeDtypeStruct(shape, kind)


def iota(shape, axis):
    return lax.broadcasted_iota(jnp.int32, shape, axis)


def picked(which, values):
    out = values[0]
    for k in range(1, len(values)):
        out = jnp.where(which == k, values[k], out)
    return out


def position():
    s, p = lax.axis_index("section"), lax.axis_index("space")
    return s, p % 2, p // 2, p


def stage_kernel(row_coef, col_coef, weight_in, weight_out, bias, gain, out, own, *scratch):
    rows, cols, biases, gains, half, taps, arrive, leave = scratch
    _, c, _, _ = position()
    start = pl.multiple_of(c * 256, 256)
    copies = [
        pltpu.make_async_copy(row_coef.at[0], rows, arrive.at[0]),
        pltpu.make_async_copy(col_coef.at[0], cols, arrive.at[1]),
        pltpu.make_async_copy(bias, biases, arrive.at[2]),
        pltpu.make_async_copy(gain, gains, arrive.at[3]),
        pltpu.make_async_copy(weight_in.at[0, :, pl.ds(start, 256)], half.at[0:256, :], arrive.at[4]),
        pltpu.make_async_copy(weight_out.at[0, pl.ds(start, 256), :], half.at[256:512, :], arrive.at[5]),
    ]
    for copy in copies:
        copy.start()
    for copy in copies[2:4]:
        copy.wait()
    line = iota((16, 256), 0)
    part = jnp.where(c == 0, biases[:, 0:256].astype(F32), biases[:, 256:512].astype(F32))
    tail = jnp.where(line == 0, part, jnp.where(line == 1, gains[...].astype(F32), 0.0))
    half[512:528, :] = tail.astype(BF16)
    for copy in copies[4:]:
        copy.wait()
    sends = [pltpu.make_async_copy(half, out.at[n], leave.at[n]) for n in range(4)]
    for copy in sends:
        copy.start()
    for copy in copies[:2]:
        copy.wait()
    zero = jnp.zeros((1, WIDE), F32)
    row, col = rows[...].astype(F32), cols[...].astype(F32)
    for m in range(4):
        taps[m] = jnp.concatenate([row[:, m, :], zero], 0).astype(BF16)
        group = jnp.concatenate([col[:, 4 * m + j, :] for j in range(4)], 1)
        taps[4 + m] = jnp.concatenate([group, zero], 0).astype(BF16)
    sends.append(pltpu.make_async_copy(taps, own, leave.at[4]))
    sends[-1].start()
    for copy in sends:
        copy.wait()


def chunk_kernel(own_taps, sib_taps, own, sib, o0, o1, o2, o3, chunk):
    _, c, z, _ = position()
    channels = own.shape[-1]
    for i in range(8):
        cells = jnp.where(c == i // 4, own[i % 4], sib[i % 4]).reshape(4, 2, COLS, channels)
        chunk[:, COLS * i : COLS * (i + 1), :] = jnp.where(c == 0, cells[:, 0], cells[:, 1])
    first, second = own_taps[0:4].astype(F32), sib_taps[0:4].astype(F32)
    taps = jnp.concatenate([jnp.where(c == 0, first, second), jnp.where(c == 0, second, first)], 0)
    turned = jnp.transpose(taps.reshape(WIDE, WIDE)).reshape(16, 8, WIDE)
    for to in range(4):
        at = [jnp.where(c == 0, turned[(4 * to + d) % 16], turned[(4 * to + d + 2) % 16]) for d in (-1, 0, 1, 2)]
        sides = [jnp.concatenate([at[1], at[2]], 0), jnp.concatenate([at[0], at[3]], 0)]
        chunk[to, GROUP : GROUP + 16, :] = jnp.concatenate(sides, 1).astype(BF16)
        edge = [jnp.where(c == 0, sib_taps[m + 6], sib_taps[m + 4]) for m in range(2)]
        chunk[to, GROUP + 16 : GROUP + 32, :] = jnp.concatenate(edge, 1)
    for k, out in enumerate((o0, o1, o2, o3)):
        out[...] = chunk[z ^ k, 0 : out.shape[0], :]


def tables_kernel(g0, g3, g2, g1, own_taps, sib_taps, taps, edges):
    _, c, z, _ = position()
    for k, g in enumerate((g0, g1, g2, g3)):
        taps[16 * k : 16 * (k + 1), :] = g[GROUP : GROUP + 16, :]
        if k != 2:
            edges[z ^ k] = g[GROUP + 16 : GROUP + 32, :]
    edge = edges[(z + 3 + 2 * c) % 4]
    for m in range(4):
        core, chip = sib_taps[4 + (m + 2) % 4], edge[:, WIDE * (m % 2) : WIDE * (m % 2 + 1)]
        margin = jnp.where(c == 0, chip, core) if m < 2 else jnp.where(c == 0, core, chip)
        taps[64 + 16 * m : 80 + 16 * m, 0:WIDE] = own_taps[4 + m]
        taps[64 + 16 * m : 80 + 16 * m, WIDE : 2 * WIDE] = margin


def field_kernel(g0, g3, g2, g1, field):
    _, _, z, _ = position()
    for k, g in enumerate((g0, g1, g2, g3)):
        field[pl.ds(pl.multiple_of((z ^ k) * GROUP, GROUP), GROUP), :] = g[0:GROUP, :]


def prepare_kernel(layers, last, q0, q3, q2, q1, *rest):
    s, c, z, p = position()
    outs, (turned, ordered, parts) = list(rest[:-3]), rest[-3:]

    tap_in, tap_out = iota((WIDE, 256), 0), iota((WIDE, 256), 1)
    expand = jnp.where((tap_in == tap_out // COLS) & (tap_in < TAPS), 1.0, 0.0).astype(BF16)
    lane, line = iota((COLS, 256), 1), iota((COLS, 256), 0)
    same = line == lane % COLS

    def columns(table, out):
        for m in range(4):
            turned[128 * m : 128 * (m + 1), :] = jnp.concatenate(
                [jnp.transpose(table[16 * m : 16 * (m + 1)]), jnp.zeros((128, WIDE - 16), F32)], 1
            )
        for i in range(ROWS):
            ordered[COLS * i : COLS * (i + 1), :] = turned[pl.ds(i, COLS, stride=ROWS), :]
        wide = jnp.dot(ordered[...].astype(BF16), expand, preferred_element_type=F32)
        for i in range(ROWS):
            row = i + lane // COLS - RADIUS
            block = jnp.where(same & (row >= 0) & (row < ROWS), wide[COLS * i : COLS * (i + 1)], 0.0)
            block = jnp.concatenate([block, jnp.zeros((COLS, CELLS - 256), F32)], 1)
            shift = (COLS * (i - RADIUS)) % CELLS
            if shift:
                block = pltpu.roll(block, shift, 1)
            out[COLS * i : COLS * (i + 1), :] = block.astype(BF16)

    lane2, line2 = iota((GROUP, WIDE), 1), iota((GROUP, WIDE), 0)
    tap = (lane2 - line2 + RADIUS + WIDE) % WIDE
    source = line2 % COLS + tap - RADIUS
    inside = (tap < TAPS) & (source >= 0) & (source < COLS)
    on_left = (tap < TAPS) & (source < 0) & (p > 0)
    on_right = (tap < TAPS) & (source >= COLS) & (p < last)
    h = line2 % COLS
    tap_u = (lane2 - line2 - 1 + WIDE) % WIDE
    tap_v = (lane2 - line2 + 15 + WIDE) % WIDE
    u_left = (h < 8) & (tap_u < TAPS) & (h + tap_u < 15)
    u_own = (h >= 8) & (tap_u < TAPS) & (h + tap_u < 15)
    v_own = (h < 8) & (tap_v < TAPS) & (h + tap_v >= 15)
    v_right = (h >= 8) & (tap_v < TAPS) & (h + tap_v >= 15)

    def rolled(part, shift):
        return jnp.concatenate([pltpu.roll(part, shift, 1, stride=1, stride_axis=0)] * 8, 0)

    def sides(left, right):
        return jnp.where(c == 0, right, left).astype(BF16), jnp.where(c == 0, left, right).astype(BF16)

    for layer in layers:
        table = picked(s ^ layer, [q[...].astype(F32) for q in (q0, q1, q2, q3)])
        columns(table[64:128, 0:WIDE], outs.pop(0))
        if layer % 2 == 0:
            columns(table[64:128, WIDE : 2 * WIDE], outs.pop(0))
        out = outs.pop(0)
        for k in range(4):
            parts[z ^ k] = table[16 * k : 16 * (k + 1)]
        for g in range(4):
            part = parts[g]
            band = rolled(part[:, 0:WIDE], WIDE - RADIUS)
            left, right = jnp.where(on_left, band, 0.0), jnp.where(on_right, band, 0.0)
            out[g, 0:GROUP, 0:WIDE] = jnp.where(inside, band, 0.0).astype(BF16)
            if layer % 2 == 1:
                margin = pltpu.roll(left, 8, 1) + pltpu.roll(right, WIDE - 8, 1)
                out[g, 0:GROUP, WIDE : 2 * WIDE] = margin.astype(BF16)
                continue
            core, chip = sides(pltpu.roll(left, 16, 1), pltpu.roll(right, WIDE - 16, 1))
            out[g, 0:GROUP, WIDE : 2 * WIDE] = core
            out[g, 0:GROUP, 2 * WIDE : 3 * WIDE] = chip
            band = rolled(part[:, WIDE : 2 * WIDE], 1)
            back = pltpu.roll(band, WIDE - 16, 1)
            mid = jnp.where(u_own, band, jnp.where(v_own, back, 0.0))
            core, chip = sides(jnp.where(u_left, band, 0.0), jnp.where(v_right, back, 0.0))
            out[g, GROUP : 2 * GROUP, 0:WIDE] = mid.astype(BF16)
            out[g, GROUP : 2 * GROUP, WIDE : 2 * WIDE] = core
            out[g, GROUP : 2 * GROUP, 2 * WIDE : 3 * WIDE] = chip


def layer_kernel(layer, fields, final, *refs):
    cells, refs = refs[:fields], refs[fields:]
    wide = fields == 3
    bands, refs = refs[0], refs[1:]
    col_bands, refs = refs[: 1 + wide], refs[1 + wide :]
    if final:
        readout, refs = refs[0], refs[1:]
    mine, theirs, refs = refs[0], refs[1], refs[2:]
    outs, rows = refs[: 1 + wide], refs[1 + wide :]
    halves = (mine.at[layer], theirs.at[layer % 2])
    channels = cells[0].shape[-1]
    for g in range(4):
        cut = slice(GROUP * g, GROUP * (g + 1))
        stacked = jnp.concatenate([x[cut] for x in cells], 0)
        done = jnp.dot(bands[g], stacked, preferred_element_type=F32).astype(BF16)
        for n, row in enumerate(rows):
            row[cut, :] = done[GROUP * n : GROUP * (n + 1)]
    size = 512
    mixed = [
        jnp.dot(band[size * b : size * (b + 1), :], row[...], preferred_element_type=F32)
        for band, row in zip(col_bands, rows)
        for b in range(CELLS // size)
    ]
    gain = halves[0][512:528, :].astype(F32)[1:2]
    for n, total in enumerate(mixed):
        inverse = lax.rsqrt(jnp.mean(total * total, axis=-1, keepdims=True) + 1e-06)
        normed = (total * inverse * gain).astype(BF16)
        parts = []
        for half in halves:
            bias = half[512:528, :].astype(F32)[0:1]
            hidden = jnp.dot(normed, half[0:256, :], preferred_element_type=F32) + bias
            inner = hidden * (0.7978845608028654 + 0.035677408136300125 * (hidden * hidden))
            hidden = 0.5 * hidden
            hidden = (hidden + hidden * jnp.tanh(inner)).astype(BF16)
            parts.append(jnp.dot(hidden, half[256:512, :], preferred_element_type=F32))
        total = (total + (parts[0] + parts[1])).astype(BF16)
        out, b = outs[n // (CELLS // size)], n % (CELLS // size)
        if final:
            reader = jnp.broadcast_to(readout[...], (8, channels))
            logit = lax.dot_general(reader, total, (((1,), (1,)), ((), ())), preferred_element_type=F32)
            logit = jnp.maximum(logit, 0.0) + jnp.log1p(jnp.exp(-jnp.abs(logit)))
            for d in range(size // 64):
                moved = pltpu.roll(logit, size - 64 * d, 1) if d else logit
                out[size // 64 * b + d : size // 64 * b + d + 1, :] = moved[0:1, 0:WIDE]
        else:
            out[size * b : size * (b + 1), :] = total


def gather_kernel(g0, g3, g2, g1, out, parts):
    _, _, z, p = position()
    for k, g in enumerate((g0, g1, g2, g3)):
        parts[z ^ k] = g[...]
    lane, line = iota((8, WIDE), 1), iota((8, WIDE), 0)
    mask = lane // COLS == line
    cells = jnp.concatenate([parts[g, core, pl.ds(p, 1), :] for g in range(4) for core in range(2)], 0)
    cells = pltpu.roll(cells, 0, 1, stride=COLS, stride_axis=0)
    for t in range(4):
        moved = pltpu.roll(cells, WIDE - COLS * t, 1) if t else cells
        out[0, t : t + 1, :] = jnp.sum(jnp.where(mask, moved, 0.0), axis=0, keepdims=True)


def window_on_section(raster, row_coef, col_coef, norm_gain, weight_in, bias_in, weight_out, readout):
    c = lax.axis_index("space") % 2
    channels = raster.shape[-1]
    spaces = lax.axis_size("space")

    def core(array):
        return lax.ppermute(array, "space", [(i, i ^ 1) for i in range(spaces)])

    def chip(array, k):
        return lax.ppermute(array, "space", [(i, i ^ (2 * k)) for i in range(spaces)])

    def section(array, k):
        return lax.ppermute(array, "section", [(i, i ^ k) for i in range(4)])

    def beside(array, ends=True):
        pairs = []
        for a in range(4):
            for q in range(spaces):
                other = q - 1 if q % 2 == 0 else q + 1
                to = a * spaces + other if 0 <= other < spaces else (a ^ 1) * spaces + q
                if ends or 0 <= other < spaces:
                    pairs.append((a * spaces + q, to))
        return lax.ppermute(array, ("section", "space"), pairs)

    window = lax.dynamic_index_in_dim(raster, lax.axis_index("section"), 0, keepdims=False)
    window_sib = core(window)
    packed, own = call(
        stage_kernel,
        (shaped((4, 528, 256)), shaped((8, 16, WIDE))),
        [ANY] * 6,
        [
            pltpu.VMEM(row_coef.shape[1:], BF16),
            pltpu.VMEM(col_coef.shape[1:], BF16),
            pltpu.VMEM((1, 512), BF16),
            pltpu.VMEM((1, 256), BF16),
            pltpu.VMEM((528, 256), BF16),
            pltpu.VMEM((8, 16, WIDE), BF16),
            pltpu.SemaphoreType.DMA((6,)),
            pltpu.SemaphoreType.DMA((5,)),
        ],
        room=56,
        place=ANY,
    )(row_coef, col_coef, weight_in, weight_out, bias_in, norm_gain)
    sib = core(own)

    chunks = call(
        chunk_kernel,
        tuple(shaped((GROUP + lines, channels)) for lines in (32, 32, 16, 32)),
        [VMEM] * 4,
        [pltpu.VMEM((4, GROUP + 32, channels), BF16)],
    )(own, sib, window, window_sib)
    sent = chunks
    chunks = [sent[0]] + [chip(sent[k], k) for k in (3, 2, 1)][::-1]

    mine = lax.all_to_all(packed, "section", split_axis=0, concat_axis=0, tiled=True)

    taps = call(
        tables_kernel, shaped((WIDE, 256)), [VMEM] * 6, [pltpu.VMEM((4, 16, 256), BF16)]
    )(chunks[0], *chunks[:0:-1], own, sib)
    field = call(field_kernel, shaped((CELLS, channels)), [VMEM] * 4)(after(chunks[0], taps), *chunks[:0:-1])
    field_core, field_chip = core(field), beside(field)
    tables = [section(taps, k) for k in (3, 2, 1)]
    tables = [taps] + tables[::-1]
    theirs = [core(after(m, *tables[::-1], field_core, field_chip)) for m in (mine[:2], mine[2:])]

    def prepare(layers, tables):
        outs = []
        for layer in layers:
            even = layer % 2 == 0
            outs += [shaped((CELLS, CELLS))] * (1 + even)
            outs.append(shaped((4, 2 * GROUP, 3 * WIDE) if even else (4, GROUP, 2 * WIDE)))
        return call(
            functools.partial(prepare_kernel, layers, spaces - 1),
            tuple(outs),
            [VMEM] * 4,
            [pltpu.VMEM((CELLS, WIDE), F32), pltpu.VMEM((CELLS, WIDE), F32), pltpu.VMEM((4, 16, 256), F32)],
        )(tables[0], *tables[:0:-1])

    def run(layer, cells, bands, readers=()):
        wide = len(cells) == 3
        final = bool(readers)
        outs = (shaped((8, WIDE), F32),) if final else (shaped((CELLS, channels)),) * (1 + wide)
        return call(
            functools.partial(layer_kernel, layer, len(cells), final),
            outs,
            [VMEM] * (len(cells) + 4 + wide + final),
            [pltpu.VMEM((CELLS, channels), BF16)] * (1 + wide),
        )(*cells, bands[-1], *bands[:-1], *readers, mine, theirs[layer // 2])

    bands0 = prepare((0,), [after(tables[0], field_chip)] + tables[1:])
    cells = run(0, (field, field_core, field_chip), bands0)
    bands1 = prepare((1,), [after(tables[0], field_chip)] + tables[1:])
    (state,) = run(1, cells, bands1)
    bands23 = prepare((2, 3), [after(t, state) for t in tables])
    cells = run(2, (state, core(state), beside(state)), bands23[:3])
    (density,) = run(3, cells, bands23[3:], (readout.reshape(1, channels),))

    beside_density = core(density)
    pair = jnp.where(c == 0, jnp.stack([density, beside_density]), jnp.stack([beside_density, density]))
    pairs = [chip(pair, k) for k in (3, 2, 1)]
    return call(
        gather_kernel, shaped((1, 4, WIDE), F32), [VMEM] * 4, [pltpu.VMEM((4, 2, 8, WIDE), F32)]
    )(pair, *pairs)


def on_device(raster, row_coef, *rest):
    fits = (
        lax.axis_size("section") == 4
        and lax.axis_size("space") == 8
        and raster.shape == (4, 4, WIDE, 256)
        and row_coef.shape[1] == TAPS
    )
    plan = window_on_section if fits else layers_over_sections
    return plan(raster, row_coef, *rest)


def solution(mesh):
    placed = (
        P(None, "space", None, None),
        P("section", None, "space", None),
        P("section", None, "space", None),
        P("section", None),
        P("section", None, None),
        P("section", None),
        P("section", None, None),
        P(),
    )
    return jax.shard_map(
        on_device,
        mesh=mesh,
        in_specs=placed,
        out_specs=P("section", "space", None),
        check_vma=False,
    )
```

```python
import functools

import jax
import jax.numpy as jnp
from jax import lax
from jax.experimental import pallas as pl
from jax.experimental.pallas import tpu as pltpu
from jax.sharding import PartitionSpec as P

F32 = jnp.float32
BF16 = jnp.bfloat16
VMEM = pl.BlockSpec(memory_space=pltpu.VMEM)
ANY = pl.BlockSpec(memory_space=pl.ANY)


def from_behind(array, axis, by):
    size = lax.axis_size(axis)
    pairs = [(i, i + by) for i in range(size) if 0 <= i + by < size]
    return lax.ppermute(array, axis, pairs)


def from_root(value, axis, source):
    kept = jnp.where(lax.axis_index(axis) == source, value, 0).astype(value.dtype)
    return lax.psum(kept, axis)


def row_stencil(surface, coefficients):
    taps_count = coefficients.shape[0]
    radius = taps_count // 2
    columns = surface.shape[1]
    padded = jnp.pad(surface.astype(F32), ((0, 0), (radius, radius), (0, 0)))
    summed = jnp.zeros(surface.shape, F32)
    for offset in range(taps_count):
        summed = (
            summed
            + coefficients[offset].astype(F32)[:, :, None] * padded[:, offset : offset + columns, :]
        )
    return summed


def col_stencil(surface, coefficients):
    taps_count = coefficients.shape[0]
    radius = taps_count // 2
    lines = surface.shape[0]
    swapped = jnp.swapaxes(coefficients, 1, 2)
    padded = jnp.pad(surface.astype(F32), ((radius, radius), (0, 0), (0, 0)))
    summed = jnp.zeros(surface.shape, F32)
    for offset in range(taps_count):
        summed = (
            summed
            + swapped[offset].astype(F32)[:, :, None] * padded[offset : offset + lines, :, :]
        )
    return summed


def apply_layer(current, params):
    row_part = row_stencil(current, params[0]).astype(BF16)
    columns_view = lax.all_to_all(row_part, "space", split_axis=1, concat_axis=0, tiled=True)
    mixed_field = col_stencil(columns_view, params[1])
    inverse = lax.rsqrt(jnp.mean(mixed_field * mixed_field, axis=-1, keepdims=True) + 1e-06)
    normed = (mixed_field * inverse * params[2].astype(F32)).astype(BF16)
    hidden = jax.nn.gelu(
        jnp.dot(normed, params[3], preferred_element_type=F32) + params[4].astype(F32),
        approximate=True,
    ).astype(BF16)
    return (mixed_field + jnp.dot(hidden, params[5], preferred_element_type=F32)).astype(BF16)


def to_rows(output):
    return lax.all_to_all(output, "space", split_axis=0, concat_axis=1, tiled=True)


def read_density(output, readout):
    return jax.nn.softplus(jnp.dot(output, readout, preferred_element_type=F32))


def layers_over_sections(
    raster, row_coef, col_coef, norm_gain, weight_in, bias_in, weight_out, readout
):
    sections = lax.axis_size("section")
    spaces = lax.axis_size("space")
    windows = raster.shape[0]
    position = lax.axis_index("section")
    params = (row_coef[0], col_coef[0], norm_gain[0], weight_in[0], bias_in[0], weight_out[0])
    carried = jnp.zeros(raster.shape[1:], BF16)
    finished = jnp.zeros((windows, raster.shape[1] * spaces, raster.shape[2] // spaces), F32)
    for moment in range(windows + sections - 1):
        entering = raster[min(moment, windows - 1)]
        current = jnp.where(position == 0, entering, carried)
        output = apply_layer(current, params)
        finished_index = moment - (sections - 1)
        if finished_index >= 0:
            finished = finished.at[finished_index].set(read_density(output, readout))
        if moment < windows + sections - 2:
            carried = from_behind(to_rows(output), "section", 1)
    row_density = lax.all_to_all(finished, "space", split_axis=1, concat_axis=2, tiled=True)
    everyone = from_root(row_density, "section", sections - 1)
    return lax.dynamic_slice_in_dim(everyone, position, 1, 0)


TAPS = 15
RADIUS = 7
ROWS = 32
COLS = 16
WIDE = 128
CELLS = ROWS * COLS
GROUP = 8 * COLS


def call(kernel, outs, specs, scratch=(), room=48, place=VMEM):
    return pl.pallas_call(
        kernel,
        out_shape=outs,
        in_specs=specs,
        out_specs=jax.tree.map(lambda _: place, outs),
        scratch_shapes=list(scratch),
        compiler_params=pltpu.CompilerParams(vmem_limit_bytes=room * 1024 * 1024),
        cost_estimate=pl.CostEstimate(flops=1, bytes_accessed=1, transcendentals=0),
    )


def after(array, *others):
    return lax.optimization_barrier((array, *others))[0]


def shaped(shape, kind=BF16):
    return jax.ShapeDtypeStruct(shape, kind)


def iota(shape, axis):
    return lax.broadcasted_iota(jnp.int32, shape, axis)


def picked(which, values):
    out = values[0]
    for k in range(1, len(values)):
        out = jnp.where(which == k, values[k], out)
    return out


def position():
    s, p = lax.axis_index("section"), lax.axis_index("space")
    return s, p % 2, p // 2, p


def stage_kernel(row_coef, col_coef, weight_in, weight_out, bias, gain, out, own, *scratch):
    rows, cols, biases, gains, half, taps, arrive, leave = scratch
    _, c, _, _ = position()
    start = pl.multiple_of(c * 256, 256)
    copies = [
        pltpu.make_async_copy(row_coef.at[0], rows, arrive.at[0]),
        pltpu.make_async_copy(col_coef.at[0], cols, arrive.at[1]),
        pltpu.make_async_copy(bias, biases, arrive.at[2]),
        pltpu.make_async_copy(gain, gains, arrive.at[3]),
        pltpu.make_async_copy(weight_in.at[0, :, pl.ds(start, 256)], half.at[0:256, :], arrive.at[4]),
        pltpu.make_async_copy(weight_out.at[0, pl.ds(start, 256), :], half.at[256:512, :], arrive.at[5]),
    ]
    for copy in copies:
        copy.start()
    for copy in copies[2:4]:
        copy.wait()
    line = iota((16, 256), 0)
    part = jnp.where(c == 0, biases[:, 0:256].astype(F32), biases[:, 256:512].astype(F32))
    tail = jnp.where(line == 0, part, jnp.where(line == 1, gains[...].astype(F32), 0.0))
    half[512:528, :] = tail.astype(BF16)
    for copy in copies[4:]:
        copy.wait()
    sends = [pltpu.make_async_copy(half, out.at[n], leave.at[n]) for n in range(4)]
    for copy in sends:
        copy.start()
    for copy in copies[:2]:
        copy.wait()
    zero = jnp.zeros((1, WIDE), F32)
    row, col = rows[...].astype(F32), cols[...].astype(F32)
    for m in range(4):
        taps[m] = jnp.concatenate([row[:, m, :], zero], 0).astype(BF16)
        group = jnp.concatenate([col[:, 4 * m + j, :] for j in range(4)], 1)
        taps[4 + m] = jnp.concatenate([group, zero], 0).astype(BF16)
    sends.append(pltpu.make_async_copy(taps, own, leave.at[4]))
    sends[-1].start()
    for copy in sends:
        copy.wait()


def chunk_kernel(own_taps, sib_taps, own, sib, o0, o1, o2, o3, chunk):
    _, c, z, _ = position()
    channels = own.shape[-1]
    for i in range(8):
        cells = jnp.where(c == i // 4, own[i % 4], sib[i % 4]).reshape(4, 2, COLS, channels)
        chunk[:, COLS * i : COLS * (i + 1), :] = jnp.where(c == 0, cells[:, 0], cells[:, 1])
    first, second = own_taps[0:4].astype(F32), sib_taps[0:4].astype(F32)
    taps = jnp.concatenate([jnp.where(c == 0, first, second), jnp.where(c == 0, second, first)], 0)
    turned = jnp.transpose(taps.reshape(WIDE, WIDE)).reshape(16, 8, WIDE)
    for to in range(4):
        at = [jnp.where(c == 0, turned[(4 * to + d) % 16], turned[(4 * to + d + 2) % 16]) for d in (-1, 0, 1, 2)]
        sides = [jnp.concatenate([at[1], at[2]], 0), jnp.concatenate([at[0], at[3]], 0)]
        chunk[to, GROUP : GROUP + 16, :] = jnp.concatenate(sides, 1).astype(BF16)
        edge = [jnp.where(c == 0, sib_taps[m + 6], sib_taps[m + 4]) for m in range(2)]
        chunk[to, GROUP + 16 : GROUP + 32, :] = jnp.concatenate(edge, 1)
    for k, out in enumerate((o0, o1, o2, o3)):
        out[...] = chunk[z ^ k, 0 : out.shape[0], :]


def tables_kernel(g0, g3, g2, g1, own_taps, sib_taps, taps, edges):
    _, c, z, _ = position()
    for k, g in enumerate((g0, g1, g2, g3)):
        taps[16 * k : 16 * (k + 1), :] = g[GROUP : GROUP + 16, :]
        if k != 2:
            edges[z ^ k] = g[GROUP + 16 : GROUP + 32, :]
    edge = edges[(z + 3 + 2 * c) % 4]
    for m in range(4):
        core, chip = sib_taps[4 + (m + 2) % 4], edge[:, WIDE * (m % 2) : WIDE * (m % 2 + 1)]
        margin = jnp.where(c == 0, chip, core) if m < 2 else jnp.where(c == 0, core, chip)
        taps[64 + 16 * m : 80 + 16 * m, 0:WIDE] = own_taps[4 + m]
        taps[64 + 16 * m : 80 + 16 * m, WIDE : 2 * WIDE] = margin


def field_kernel(g0, g3, g2, g1, field):
    _, _, z, _ = position()
    for k, g in enumerate((g0, g1, g2, g3)):
        field[pl.ds(pl.multiple_of((z ^ k) * GROUP, GROUP), GROUP), :] = g[0:GROUP, :]


def prepare_kernel(layers, last, q0, q3, q2, q1, *rest):
    s, c, z, p = position()
    outs, (turned, ordered, parts) = list(rest[:-3]), rest[-3:]

    tap_in, tap_out = iota((WIDE, 256), 0), iota((WIDE, 256), 1)
    expand = jnp.where((tap_in == tap_out // COLS) & (tap_in < TAPS), 1.0, 0.0).astype(BF16)
    lane, line = iota((COLS, 256), 1), iota((COLS, 256), 0)
    same = line == lane % COLS

    def columns(table, out):
        for m in range(4):
            turned[128 * m : 128 * (m + 1), :] = jnp.concatenate(
                [jnp.transpose(table[16 * m : 16 * (m + 1)]), jnp.zeros((128, WIDE - 16), F32)], 1
            )
        for i in range(ROWS):
            ordered[COLS * i : COLS * (i + 1), :] = turned[pl.ds(i, COLS, stride=ROWS), :]
        wide = jnp.dot(ordered[...].astype(BF16), expand, preferred_element_type=F32)
        for i in range(ROWS):
            row = i + lane // COLS - RADIUS
            block = jnp.where(same & (row >= 0) & (row < ROWS), wide[COLS * i : COLS * (i + 1)], 0.0)
            block = jnp.concatenate([block, jnp.zeros((COLS, CELLS - 256), F32)], 1)
            shift = (COLS * (i - RADIUS)) % CELLS
            if shift:
                block = pltpu.roll(block, shift, 1)
            out[COLS * i : COLS * (i + 1), :] = block.astype(BF16)

    lane2, line2 = iota((GROUP, WIDE), 1), iota((GROUP, WIDE), 0)
    tap = (lane2 - line2 + RADIUS + WIDE) % WIDE
    source = line2 % COLS + tap - RADIUS
    inside = (tap < TAPS) & (source >= 0) & (source < COLS)
    on_left = (tap < TAPS) & (source < 0) & (p > 0)
    on_right = (tap < TAPS) & (source >= COLS) & (p < last)
    h = line2 % COLS
    tap_u = (lane2 - line2 - 1 + WIDE) % WIDE
    tap_v = (lane2 - line2 + 15 + WIDE) % WIDE
    u_left = (h < 8) & (tap_u < TAPS) & (h + tap_u < 15)
    u_own = (h >= 8) & (tap_u < TAPS) & (h + tap_u < 15)
    v_own = (h < 8) & (tap_v < TAPS) & (h + tap_v >= 15)
    v_right = (h >= 8) & (tap_v < TAPS) & (h + tap_v >= 15)

    def rolled(part, shift):
        return jnp.concatenate([pltpu.roll(part, shift, 1, stride=1, stride_axis=0)] * 8, 0)

    def sides(left, right):
        return jnp.where(c == 0, right, left).astype(BF16), jnp.where(c == 0, left, right).astype(BF16)

    for layer in layers:
        table = picked(s ^ layer, [q[...].astype(F32) for q in (q0, q1, q2, q3)])
        columns(table[64:128, 0:WIDE], outs.pop(0))
        if layer % 2 == 0:
            columns(table[64:128, WIDE : 2 * WIDE], outs.pop(0))
        out = outs.pop(0)
        for k in range(4):
            parts[z ^ k] = table[16 * k : 16 * (k + 1)]
        for g in range(4):
            part = parts[g]
            band = rolled(part[:, 0:WIDE], WIDE - RADIUS)
            left, right = jnp.where(on_left, band, 0.0), jnp.where(on_right, band, 0.0)
            out[g, 0:GROUP, 0:WIDE] = jnp.where(inside, band, 0.0).astype(BF16)
            if layer % 2 == 1:
                margin = pltpu.roll(left, 8, 1) + pltpu.roll(right, WIDE - 8, 1)
                out[g, 0:GROUP, WIDE : 2 * WIDE] = margin.astype(BF16)
                continue
            core, chip = sides(pltpu.roll(left, 16, 1), pltpu.roll(right, WIDE - 16, 1))
            out[g, 0:GROUP, WIDE : 2 * WIDE] = core
            out[g, 0:GROUP, 2 * WIDE : 3 * WIDE] = chip
            band = rolled(part[:, WIDE : 2 * WIDE], 1)
            back = pltpu.roll(band, WIDE - 16, 1)
            mid = jnp.where(u_own, band, jnp.where(v_own, back, 0.0))
            core, chip = sides(jnp.where(u_left, band, 0.0), jnp.where(v_right, back, 0.0))
            out[g, GROUP : 2 * GROUP, 0:WIDE] = mid.astype(BF16)
            out[g, GROUP : 2 * GROUP, WIDE : 2 * WIDE] = core
            out[g, GROUP : 2 * GROUP, 2 * WIDE : 3 * WIDE] = chip


def layer_kernel(layer, fields, final, *refs):
    cells, refs = refs[:fields], refs[fields:]
    wide = fields == 3
    bands, refs = refs[0], refs[1:]
    col_bands, refs = refs[: 1 + wide], refs[1 + wide :]
    if final:
        readout, refs = refs[0], refs[1:]
    mine, theirs, refs = refs[0], refs[1], refs[2:]
    outs, rows = refs[: 1 + wide], refs[1 + wide :]
    halves = (mine.at[layer], theirs.at[layer % 2])
    channels = cells[0].shape[-1]
    for g in range(4):
        cut = slice(GROUP * g, GROUP * (g + 1))
        stacked = jnp.concatenate([x[cut] for x in cells], 0)
        done = jnp.dot(bands[g], stacked, preferred_element_type=F32).astype(BF16)
        for n, row in enumerate(rows):
            row[cut, :] = done[GROUP * n : GROUP * (n + 1)]
    size = 512
    mixed = [
        jnp.dot(band[size * b : size * (b + 1), :], row[...], preferred_element_type=F32)
        for band, row in zip(col_bands, rows)
        for b in range(CELLS // size)
    ]
    gain = halves[0][512:528, :].astype(F32)[1:2]
    bias = jnp.concatenate([half[512:528, :].astype(F32)[0:1] for half in halves], 1)
    weight_in = jnp.concatenate([half[0:256, :] for half in halves], 1)
    weight_out = jnp.concatenate([half[256:512, :] for half in halves], 0)
    for n, total in enumerate(mixed):
        inverse = lax.rsqrt(jnp.mean(total * total, axis=-1, keepdims=True) + 1e-06)
        normed = (total * inverse * gain).astype(BF16)
        hidden = jnp.dot(normed, weight_in, preferred_element_type=F32) + bias
        inner = hidden * (0.7978845608028654 + 0.035677408136300125 * (hidden * hidden))
        hidden = (hidden + hidden * jnp.tanh(inner)).astype(BF16)
        total = (total + 0.5 * jnp.dot(hidden, weight_out, preferred_element_type=F32)).astype(BF16)
        out, b = outs[n // (CELLS // size)], n % (CELLS // size)
        if final:
            reader = jnp.broadcast_to(readout[...], (8, channels))
            logit = lax.dot_general(reader, total, (((1,), (1,)), ((), ())), preferred_element_type=F32)
            logit = jnp.maximum(logit, 0.0) + jnp.log1p(jnp.exp(-jnp.abs(logit)))
            for d in range(size // 64):
                moved = pltpu.roll(logit, size - 64 * d, 1) if d else logit
                out[size // 64 * b + d : size // 64 * b + d + 1, :] = moved[0:1, 0:WIDE]
        else:
            out[size * b : size * (b + 1), :] = total


def gather_kernel(g0, g3, g2, g1, out, parts):
    _, _, z, p = position()
    for k, g in enumerate((g0, g1, g2, g3)):
        parts[z ^ k] = g[...]
    lane, line = iota((8, WIDE), 1), iota((8, WIDE), 0)
    mask = lane // COLS == line
    cells = jnp.concatenate([parts[g, core, pl.ds(p, 1), :] for g in range(4) for core in range(2)], 0)
    cells = pltpu.roll(cells, 0, 1, stride=COLS, stride_axis=0)
    for t in range(4):
        moved = pltpu.roll(cells, WIDE - COLS * t, 1) if t else cells
        out[0, t : t + 1, :] = jnp.sum(jnp.where(mask, moved, 0.0), axis=0, keepdims=True)


def window_on_section(raster, row_coef, col_coef, norm_gain, weight_in, bias_in, weight_out, readout):
    c = lax.axis_index("space") % 2
    channels = raster.shape[-1]
    spaces = lax.axis_size("space")

    def core(array):
        return lax.ppermute(array, "space", [(i, i ^ 1) for i in range(spaces)])

    def chip(array, k):
        return lax.ppermute(array, "space", [(i, i ^ (2 * k)) for i in range(spaces)])

    def section(array, k):
        return lax.ppermute(array, "section", [(i, i ^ k) for i in range(4)])

    def beside(array, ends=True):
        pairs = []
        for a in range(4):
            for q in range(spaces):
                other = q - 1 if q % 2 == 0 else q + 1
                to = a * spaces + other if 0 <= other < spaces else (a ^ 1) * spaces + q
                if ends or 0 <= other < spaces:
                    pairs.append((a * spaces + q, to))
        return lax.ppermute(array, ("section", "space"), pairs)

    window = lax.dynamic_index_in_dim(raster, lax.axis_index("section"), 0, keepdims=False)
    window_sib = core(window)
    packed, own = call(
        stage_kernel,
        (shaped((4, 528, 256)), shaped((8, 16, WIDE))),
        [ANY] * 6,
        [
            pltpu.VMEM(row_coef.shape[1:], BF16),
            pltpu.VMEM(col_coef.shape[1:], BF16),
            pltpu.VMEM((1, 512), BF16),
            pltpu.VMEM((1, 256), BF16),
            pltpu.VMEM((528, 256), BF16),
            pltpu.VMEM((8, 16, WIDE), BF16),
            pltpu.SemaphoreType.DMA((6,)),
            pltpu.SemaphoreType.DMA((5,)),
        ],
        room=56,
        place=ANY,
    )(row_coef, col_coef, weight_in, weight_out, bias_in, norm_gain)
    sib = core(own)

    chunks = call(
        chunk_kernel,
        tuple(shaped((GROUP + lines, channels)) for lines in (32, 32, 16, 32)),
        [VMEM] * 4,
        [pltpu.VMEM((4, GROUP + 32, channels), BF16)],
    )(own, sib, window, window_sib)
    sent = chunks
    chunks = [sent[0]] + [chip(sent[k], k) for k in (3, 2, 1)][::-1]

    mine = lax.all_to_all(packed, "section", split_axis=0, concat_axis=0, tiled=True)

    taps = call(
        tables_kernel, shaped((WIDE, 256)), [VMEM] * 6, [pltpu.VMEM((4, 16, 256), BF16)]
    )(chunks[0], *chunks[:0:-1], own, sib)
    field = call(field_kernel, shaped((CELLS, channels)), [VMEM] * 4)(after(chunks[0], taps), *chunks[:0:-1])
    field_core, field_chip = core(field), beside(field)
    tables = [section(taps, k) for k in (3, 2, 1)]
    tables = [taps] + tables[::-1]
    theirs = [core(after(m, *tables[::-1], field_core, field_chip)) for m in (mine[:2], mine[2:])]

    def prepare(layers, tables):
        outs = []
        for layer in layers:
            even = layer % 2 == 0
            outs += [shaped((CELLS, CELLS))] * (1 + even)
            outs.append(shaped((4, 2 * GROUP, 3 * WIDE) if even else (4, GROUP, 2 * WIDE)))
        return call(
            functools.partial(prepare_kernel, layers, spaces - 1),
            tuple(outs),
            [VMEM] * 4,
            [pltpu.VMEM((CELLS, WIDE), F32), pltpu.VMEM((CELLS, WIDE), F32), pltpu.VMEM((4, 16, 256), F32)],
        )(tables[0], *tables[:0:-1])

    def run(layer, cells, bands, readers=()):
        wide = len(cells) == 3
        final = bool(readers)
        outs = (shaped((8, WIDE), F32),) if final else (shaped((CELLS, channels)),) * (1 + wide)
        return call(
            functools.partial(layer_kernel, layer, len(cells), final),
            outs,
            [VMEM] * (len(cells) + 4 + wide + final),
            [pltpu.VMEM((CELLS, channels), BF16)] * (1 + wide),
        )(*cells, bands[-1], *bands[:-1], *readers, mine, theirs[layer // 2])

    bands0 = prepare((0,), [after(tables[0], field_chip)] + tables[1:])
    cells = run(0, (field, field_core, field_chip), bands0)
    bands1 = prepare((1,), [after(tables[0], field_chip)] + tables[1:])
    (state,) = run(1, cells, bands1)
    bands23 = prepare((2, 3), [after(t, state) for t in tables])
    cells = run(2, (state, core(state), beside(state)), bands23[:3])
    (density,) = run(3, cells, bands23[3:], (readout.reshape(1, channels),))

    beside_density = core(density)
    pair = jnp.where(c == 0, jnp.stack([density, beside_density]), jnp.stack([beside_density, density]))
    pairs = [chip(pair, k) for k in (3, 2, 1)]
    return call(
        gather_kernel, shaped((1, 4, WIDE), F32), [VMEM] * 4, [pltpu.VMEM((4, 2, 8, WIDE), F32)]
    )(pair, *pairs)


def on_device(raster, row_coef, *rest):
    fits = (
        lax.axis_size("section") == 4
        and lax.axis_size("space") == 8
        and raster.shape == (4, 4, WIDE, 256)
        and row_coef.shape[1] == TAPS
    )
    plan = window_on_section if fits else layers_over_sections
    return plan(raster, row_coef, *rest)


def solution(mesh):
    placed = (
        P(None, "space", None, None),
        P("section", None, "space", None),
        P("section", None, "space", None),
        P("section", None),
        P("section", None, None),
        P("section", None),
        P("section", None, None),
        P(),
    )
    return jax.shard_map(
        on_device,
        mesh=mesh,
        in_specs=placed,
        out_specs=P("section", "space", None),
        check_vma=False,
    )
```

```python
import functools

import jax
import jax.numpy as jnp
from jax import lax
from jax.experimental import pallas as pl
from jax.experimental.pallas import tpu as pltpu
from jax.sharding import PartitionSpec as P

F32 = jnp.float32
BF16 = jnp.bfloat16
VMEM = pl.BlockSpec(memory_space=pltpu.VMEM)
ANY = pl.BlockSpec(memory_space=pl.ANY)


def from_behind(array, axis, by):
    size = lax.axis_size(axis)
    pairs = [(i, i + by) for i in range(size) if 0 <= i + by < size]
    return lax.ppermute(array, axis, pairs)


def from_root(value, axis, source):
    kept = jnp.where(lax.axis_index(axis) == source, value, 0).astype(value.dtype)
    return lax.psum(kept, axis)


def row_stencil(surface, coefficients):
    taps_count = coefficients.shape[0]
    radius = taps_count // 2
    columns = surface.shape[1]
    padded = jnp.pad(surface.astype(F32), ((0, 0), (radius, radius), (0, 0)))
    summed = jnp.zeros(surface.shape, F32)
    for offset in range(taps_count):
        summed = (
            summed
            + coefficients[offset].astype(F32)[:, :, None] * padded[:, offset : offset + columns, :]
        )
    return summed


def col_stencil(surface, coefficients):
    taps_count = coefficients.shape[0]
    radius = taps_count // 2
    lines = surface.shape[0]
    swapped = jnp.swapaxes(coefficients, 1, 2)
    padded = jnp.pad(surface.astype(F32), ((radius, radius), (0, 0), (0, 0)))
    summed = jnp.zeros(surface.shape, F32)
    for offset in range(taps_count):
        summed = (
            summed
            + swapped[offset].astype(F32)[:, :, None] * padded[offset : offset + lines, :, :]
        )
    return summed


def apply_layer(current, params):
    row_part = row_stencil(current, params[0]).astype(BF16)
    columns_view = lax.all_to_all(row_part, "space", split_axis=1, concat_axis=0, tiled=True)
    mixed_field = col_stencil(columns_view, params[1])
    inverse = lax.rsqrt(jnp.mean(mixed_field * mixed_field, axis=-1, keepdims=True) + 1e-06)
    normed = (mixed_field * inverse * params[2].astype(F32)).astype(BF16)
    hidden = jax.nn.gelu(
        jnp.dot(normed, params[3], preferred_element_type=F32) + params[4].astype(F32),
        approximate=True,
    ).astype(BF16)
    return (mixed_field + jnp.dot(hidden, params[5], preferred_element_type=F32)).astype(BF16)


def to_rows(output):
    return lax.all_to_all(output, "space", split_axis=0, concat_axis=1, tiled=True)


def read_density(output, readout):
    return jax.nn.softplus(jnp.dot(output, readout, preferred_element_type=F32))


def layers_over_sections(
    raster, row_coef, col_coef, norm_gain, weight_in, bias_in, weight_out, readout
):
    sections = lax.axis_size("section")
    spaces = lax.axis_size("space")
    windows = raster.shape[0]
    position = lax.axis_index("section")
    params = (row_coef[0], col_coef[0], norm_gain[0], weight_in[0], bias_in[0], weight_out[0])
    carried = jnp.zeros(raster.shape[1:], BF16)
    finished = jnp.zeros((windows, raster.shape[1] * spaces, raster.shape[2] // spaces), F32)
    for moment in range(windows + sections - 1):
        entering = raster[min(moment, windows - 1)]
        current = jnp.where(position == 0, entering, carried)
        output = apply_layer(current, params)
        finished_index = moment - (sections - 1)
        if finished_index >= 0:
            finished = finished.at[finished_index].set(read_density(output, readout))
        if moment < windows + sections - 2:
            carried = from_behind(to_rows(output), "section", 1)
    row_density = lax.all_to_all(finished, "space", split_axis=1, concat_axis=2, tiled=True)
    everyone = from_root(row_density, "section", sections - 1)
    return lax.dynamic_slice_in_dim(everyone, position, 1, 0)


TAPS = 15
RADIUS = 7
ROWS = 32
COLS = 16
WIDE = 128
CELLS = ROWS * COLS
GROUP = 8 * COLS


def call(kernel, outs, specs, scratch=(), room=48, place=VMEM):
    return pl.pallas_call(
        kernel,
        out_shape=outs,
        in_specs=specs,
        out_specs=jax.tree.map(lambda _: place, outs),
        scratch_shapes=list(scratch),
        compiler_params=pltpu.CompilerParams(vmem_limit_bytes=room * 1024 * 1024),
        cost_estimate=pl.CostEstimate(flops=1, bytes_accessed=1, transcendentals=0),
    )


def after(array, *others):
    return lax.optimization_barrier((array, *others))[0]


def shaped(shape, kind=BF16):
    return jax.ShapeDtypeStruct(shape, kind)


def iota(shape, axis):
    return lax.broadcasted_iota(jnp.int32, shape, axis)


def picked(which, values):
    out = values[0]
    for k in range(1, len(values)):
        out = jnp.where(which == k, values[k], out)
    return out


def position():
    s, p = lax.axis_index("section"), lax.axis_index("space")
    return s, p % 2, p // 2, p


def stage_kernel(row_coef, col_coef, weight_in, weight_out, bias, gain, out, own, *scratch):
    rows, cols, biases, gains, half, taps, arrive, leave = scratch
    _, c, _, _ = position()
    start = pl.multiple_of(c * 256, 256)
    copies = [
        pltpu.make_async_copy(row_coef.at[0], rows, arrive.at[0]),
        pltpu.make_async_copy(col_coef.at[0], cols, arrive.at[1]),
        pltpu.make_async_copy(bias, biases, arrive.at[2]),
        pltpu.make_async_copy(gain, gains, arrive.at[3]),
        pltpu.make_async_copy(weight_in.at[0, :, pl.ds(start, 256)], half.at[0:256, :], arrive.at[4]),
        pltpu.make_async_copy(weight_out.at[0, pl.ds(start, 256), :], half.at[256:512, :], arrive.at[5]),
    ]
    for copy in copies:
        copy.start()
    for copy in copies[:4]:
        copy.wait()
    line = iota((16, 256), 0)
    part = jnp.where(c == 0, biases[:, 0:256].astype(F32), biases[:, 256:512].astype(F32))
    tail = jnp.where(line == 0, part, jnp.where(line == 1, gains[...].astype(F32), 0.0))
    half[512:528, :] = tail.astype(BF16)
    zero = jnp.zeros((1, WIDE), F32)
    row, col = rows[...].astype(F32), cols[...].astype(F32)
    for m in range(4):
        taps[m] = jnp.concatenate([row[:, m, :], zero], 0).astype(BF16)
        group = jnp.concatenate([col[:, 4 * m + j, :] for j in range(4)], 1)
        group = jnp.concatenate([group, zero], 0).astype(BF16)
        taps[4 + m] = group
        half[528 + 16 * (m // 2) : 544 + 16 * (m // 2), WIDE * (m % 2) : WIDE * (m % 2 + 1)] = group
    for copy in copies[4:]:
        copy.wait()
    sends = [pltpu.make_async_copy(half, out.at[n], leave.at[n]) for n in range(4)]
    sends.append(pltpu.make_async_copy(taps, own, leave.at[4]))
    for copy in sends:
        copy.start()
    for copy in sends:
        copy.wait()


def chunk_kernel(own_taps, sib_taps, own, sib, o0, o1, o2, o3, chunk):
    _, c, z, _ = position()
    channels = own.shape[-1]
    for i in range(8):
        cells = jnp.where(c == i // 4, own[i % 4], sib[i % 4]).reshape(4, 2, COLS, channels)
        chunk[:, COLS * i : COLS * (i + 1), :] = jnp.where(c == 0, cells[:, 0], cells[:, 1])
    first, second = own_taps[0:4].astype(F32), sib_taps[0:4].astype(F32)
    taps = jnp.concatenate([jnp.where(c == 0, first, second), jnp.where(c == 0, second, first)], 0)
    turned = jnp.transpose(taps.reshape(WIDE, WIDE)).reshape(16, 8, WIDE)
    for to in range(4):
        at = [jnp.where(c == 0, turned[(4 * to + d) % 16], turned[(4 * to + d + 2) % 16]) for d in (-1, 0, 1, 2)]
        sides = [jnp.concatenate([at[1], at[2]], 0), jnp.concatenate([at[0], at[3]], 0)]
        chunk[to, GROUP : GROUP + 16, :] = jnp.concatenate(sides, 1).astype(BF16)
        edge = [jnp.where(c == 0, sib_taps[m + 6], sib_taps[m + 4]) for m in range(2)]
        chunk[to, GROUP + 16 : GROUP + 32, :] = jnp.concatenate(edge, 1)
    for k, out in enumerate((o0, o1, o2, o3)):
        out[...] = chunk[z ^ k, 0 : out.shape[0], :]


def tables_kernel(g0, g3, g2, g1, sib_taps, taps, edges):
    _, c, z, _ = position()
    for k, g in enumerate((g0, g1, g2, g3)):
        taps[16 * k : 16 * (k + 1), :] = g[GROUP : GROUP + 16, :]
        if k != 2:
            edges[z ^ k] = g[GROUP + 16 : GROUP + 32, :]
    chip = edges[(z + 3 + 2 * c) % 4]
    for n in range(2):
        core = jnp.concatenate([sib_taps[4 + (2 * n + m + 2) % 4] for m in range(2)], 1)
        left = c == n
        taps[64 + 16 * n : 80 + 16 * n, :] = jnp.where(left, chip, core)


def field_kernel(g0, g3, g2, g1, field):
    _, _, z, _ = position()
    for k, g in enumerate((g0, g1, g2, g3)):
        field[pl.ds(pl.multiple_of((z ^ k) * GROUP, GROUP), GROUP), :] = g[0:GROUP, :]


def columns(groups, out, turned, ordered):
    tap_in, tap_out = iota((WIDE, 256), 0), iota((WIDE, 256), 1)
    expand = jnp.where((tap_in == tap_out // COLS) & (tap_in < TAPS), 1.0, 0.0).astype(BF16)
    lane, line = iota((COLS, 256), 1), iota((COLS, 256), 0)
    same = line == lane % COLS
    for m, group in enumerate(groups):
        turned[128 * m : 128 * (m + 1), :] = jnp.concatenate(
            [jnp.transpose(group), jnp.zeros((128, WIDE - 16), F32)], 1
        )
    for i in range(ROWS):
        ordered[COLS * i : COLS * (i + 1), :] = turned[pl.ds(i, COLS, stride=ROWS), :]
    wide = jnp.dot(ordered[...].astype(BF16), expand, preferred_element_type=F32)
    for i in range(ROWS):
        row = i + lane // COLS - RADIUS
        block = jnp.where(same & (row >= 0) & (row < ROWS), wide[COLS * i : COLS * (i + 1)], 0.0)
        block = jnp.concatenate([block, jnp.zeros((COLS, CELLS - 256), F32)], 1)
        shift = (COLS * (i - RADIUS)) % CELLS
        if shift:
            block = pltpu.roll(block, shift, 1)
        out[COLS * i : COLS * (i + 1), :] = block.astype(BF16)


def own_columns_kernel(layers, weights, *rest):
    outs, scratch = rest[:-2], rest[-2:]
    for layer, out in zip(layers, outs):
        table = weights[layer, 528:560, :].astype(F32)
        groups = [table[16 * n : 16 * (n + 1), WIDE * m : WIDE * (m + 1)] for n in range(2) for m in range(2)]
        columns(groups, out, *scratch)


def prepare_kernel(layers, last, q0, q3, q2, q1, *rest):
    s, c, z, p = position()
    outs, (turned, ordered, parts) = list(rest[:-3]), rest[-3:]

    lane2, line2 = iota((GROUP, WIDE), 1), iota((GROUP, WIDE), 0)
    tap = (lane2 - line2 + RADIUS + WIDE) % WIDE
    source = line2 % COLS + tap - RADIUS
    inside = (tap < TAPS) & (source >= 0) & (source < COLS)
    on_left = (tap < TAPS) & (source < 0) & (p > 0)
    on_right = (tap < TAPS) & (source >= COLS) & (p < last)
    h = line2 % COLS
    tap_u = (lane2 - line2 - 1 + WIDE) % WIDE
    tap_v = (lane2 - line2 + 15 + WIDE) % WIDE
    u_left = (h < 8) & (tap_u < TAPS) & (h + tap_u < 15)
    u_own = (h >= 8) & (tap_u < TAPS) & (h + tap_u < 15)
    v_own = (h < 8) & (tap_v < TAPS) & (h + tap_v >= 15)
    v_right = (h >= 8) & (tap_v < TAPS) & (h + tap_v >= 15)

    def rolled(part, shift):
        return jnp.concatenate([pltpu.roll(part, shift, 1, stride=1, stride_axis=0)] * 8, 0)

    def sides(left, right):
        return jnp.where(c == 0, right, left).astype(BF16), jnp.where(c == 0, left, right).astype(BF16)

    for layer in layers:
        table = picked(s ^ layer, [q[...].astype(F32) for q in (q0, q1, q2, q3)])
        if layer % 2 == 0:
            margin = table[64:96]
            groups = [margin[16 * n : 16 * (n + 1), WIDE * m : WIDE * (m + 1)] for n in range(2) for m in range(2)]
            columns(groups, outs.pop(0), turned, ordered)
        out = outs.pop(0)
        for k in range(4):
            parts[z ^ k] = table[16 * k : 16 * (k + 1)]
        for g in range(4):
            part = parts[g]
            band = rolled(part[:, 0:WIDE], WIDE - RADIUS)
            left, right = jnp.where(on_left, band, 0.0), jnp.where(on_right, band, 0.0)
            out[g, 0:GROUP, 0:WIDE] = jnp.where(inside, band, 0.0).astype(BF16)
            if layer % 2 == 1:
                margin = pltpu.roll(left, 8, 1) + pltpu.roll(right, WIDE - 8, 1)
                out[g, 0:GROUP, WIDE : 2 * WIDE] = margin.astype(BF16)
                continue
            core, chip = sides(pltpu.roll(left, 16, 1), pltpu.roll(right, WIDE - 16, 1))
            out[g, 0:GROUP, WIDE : 2 * WIDE] = core
            out[g, 0:GROUP, 2 * WIDE : 3 * WIDE] = chip
            band = rolled(part[:, WIDE : 2 * WIDE], 1)
            back = pltpu.roll(band, WIDE - 16, 1)
            mid = jnp.where(u_own, band, jnp.where(v_own, back, 0.0))
            core, chip = sides(jnp.where(u_left, band, 0.0), jnp.where(v_right, back, 0.0))
            out[g, GROUP : 2 * GROUP, 0:WIDE] = mid.astype(BF16)
            out[g, GROUP : 2 * GROUP, WIDE : 2 * WIDE] = core
            out[g, GROUP : 2 * GROUP, 2 * WIDE : 3 * WIDE] = chip


def layer_kernel(layer, fields, final, *refs):
    cells, refs = refs[:fields], refs[fields:]
    wide = fields == 3
    bands, refs = refs[0], refs[1:]
    col_bands, refs = refs[: 1 + wide], refs[1 + wide :]
    if final:
        readout, refs = refs[0], refs[1:]
    mine, theirs, refs = refs[0], refs[1], refs[2:]
    outs, rows = refs[: 1 + wide], refs[1 + wide :]
    halves = (mine.at[layer], theirs.at[layer % 2])
    channels = cells[0].shape[-1]
    for g in range(4):
        cut = slice(GROUP * g, GROUP * (g + 1))
        stacked = jnp.concatenate([x[cut] for x in cells], 0)
        done = jnp.dot(bands[g], stacked, preferred_element_type=F32).astype(BF16)
        for n, row in enumerate(rows):
            row[cut, :] = done[GROUP * n : GROUP * (n + 1)]
    size = 512
    mixed = [
        jnp.dot(band[size * b : size * (b + 1), :], row[...], preferred_element_type=F32)
        for band, row in zip(col_bands, rows)
        for b in range(CELLS // size)
    ]
    gain = halves[0][512:528, :].astype(F32)[1:2]
    bias = jnp.concatenate([half[512:528, :].astype(F32)[0:1] for half in halves], 1)
    weight_in = jnp.concatenate([half[0:256, :] for half in halves], 1)
    weight_out = jnp.concatenate([half[256:512, :] for half in halves], 0)
    for n, total in enumerate(mixed):
        inverse = lax.rsqrt(jnp.mean(total * total, axis=-1, keepdims=True) + 1e-06)
        normed = (total * inverse * gain).astype(BF16)
        hidden = jnp.dot(normed, weight_in, preferred_element_type=F32) + bias
        inner = hidden * (0.7978845608028654 + 0.035677408136300125 * (hidden * hidden))
        hidden = (hidden + hidden * jnp.tanh(inner)).astype(BF16)
        total = (total + 0.5 * jnp.dot(hidden, weight_out, preferred_element_type=F32)).astype(BF16)
        out, b = outs[n // (CELLS // size)], n % (CELLS // size)
        if final:
            reader = jnp.broadcast_to(readout[...], (8, channels))
            logit = lax.dot_general(reader, total, (((1,), (1,)), ((), ())), preferred_element_type=F32)
            logit = jnp.maximum(logit, 0.0) + jnp.log1p(jnp.exp(-jnp.abs(logit)))
            for d in range(size // 64):
                moved = pltpu.roll(logit, size - 64 * d, 1) if d else logit
                out[size // 64 * b + d : size // 64 * b + d + 1, :] = moved[0:1, 0:WIDE]
        else:
            out[size * b : size * (b + 1), :] = total


def gather_kernel(g0, g3, g2, g1, out, parts):
    _, _, z, p = position()
    for k, g in enumerate((g0, g1, g2, g3)):
        parts[z ^ k] = g[...]
    lane, line = iota((8, WIDE), 1), iota((8, WIDE), 0)
    mask = lane // COLS == line
    cells = jnp.concatenate([parts[g, core, pl.ds(p, 1), :] for g in range(4) for core in range(2)], 0)
    cells = pltpu.roll(cells, 0, 1, stride=COLS, stride_axis=0)
    for t in range(4):
        moved = pltpu.roll(cells, WIDE - COLS * t, 1) if t else cells
        out[0, t : t + 1, :] = jnp.sum(jnp.where(mask, moved, 0.0), axis=0, keepdims=True)


def window_on_section(raster, row_coef, col_coef, norm_gain, weight_in, bias_in, weight_out, readout):
    c = lax.axis_index("space") % 2
    channels = raster.shape[-1]
    spaces = lax.axis_size("space")

    def core(array):
        return lax.ppermute(array, "space", [(i, i ^ 1) for i in range(spaces)])

    def chip(array, k):
        return lax.ppermute(array, "space", [(i, i ^ (2 * k)) for i in range(spaces)])

    def section(array, k):
        return lax.ppermute(array, "section", [(i, i ^ k) for i in range(4)])

    def beside(array, ends=True):
        pairs = []
        for a in range(4):
            for q in range(spaces):
                other = q - 1 if q % 2 == 0 else q + 1
                to = a * spaces + other if 0 <= other < spaces else (a ^ 1) * spaces + q
                if ends or 0 <= other < spaces:
                    pairs.append((a * spaces + q, to))
        return lax.ppermute(array, ("section", "space"), pairs)

    window = lax.dynamic_index_in_dim(raster, lax.axis_index("section"), 0, keepdims=False)
    window_sib = core(window)
    packed, own = call(
        stage_kernel,
        (shaped((4, 560, 256)), shaped((8, 16, WIDE))),
        [ANY] * 6,
        [
            pltpu.VMEM(row_coef.shape[1:], BF16),
            pltpu.VMEM(col_coef.shape[1:], BF16),
            pltpu.VMEM((1, 512), BF16),
            pltpu.VMEM((1, 256), BF16),
            pltpu.VMEM((560, 256), BF16),
            pltpu.VMEM((8, 16, WIDE), BF16),
            pltpu.SemaphoreType.DMA((6,)),
            pltpu.SemaphoreType.DMA((5,)),
        ],
        room=56,
        place=ANY,
    )(row_coef, col_coef, weight_in, weight_out, bias_in, norm_gain)
    sib = core(own)

    chunks = call(
        chunk_kernel,
        tuple(shaped((GROUP + lines, channels)) for lines in (32, 32, 16, 32)),
        [VMEM] * 4,
        [pltpu.VMEM((4, GROUP + 32, channels), BF16)],
    )(own, sib, window, window_sib)
    sent = chunks
    chunks = [sent[0]] + [chip(sent[k], k) for k in (3, 2, 1)][::-1]

    mine = lax.all_to_all(packed, "section", split_axis=0, concat_axis=0, tiled=True)

    taps = call(
        tables_kernel, shaped((96, 256)), [VMEM] * 5, [pltpu.VMEM((4, 16, 256), BF16)]
    )(chunks[0], *chunks[:0:-1], sib)
    field = call(field_kernel, shaped((CELLS, channels)), [VMEM] * 4)(after(chunks[0], taps), *chunks[:0:-1])
    field_core, field_chip = core(field), beside(field)
    tables = [section(taps, k) for k in (3, 2, 1)]
    tables = [taps] + tables[::-1]
    def prepare(layers, tables):
        outs = []
        for layer in layers:
            even = layer % 2 == 0
            outs += [shaped((CELLS, CELLS))] * even
            outs.append(shaped((4, 2 * GROUP, 3 * WIDE) if even else (4, GROUP, 2 * WIDE)))
        return call(
            functools.partial(prepare_kernel, layers, spaces - 1),
            tuple(outs),
            [VMEM] * 4,
            [pltpu.VMEM((CELLS, WIDE), F32), pltpu.VMEM((CELLS, WIDE), F32), pltpu.VMEM((4, 16, 256), F32)],
        )(tables[0], *tables[:0:-1])

    def own_columns(layers, weights):
        return call(
            functools.partial(own_columns_kernel, layers),
            (shaped((CELLS, CELLS)),) * len(layers),
            [VMEM],
            [pltpu.VMEM((CELLS, WIDE), F32), pltpu.VMEM((CELLS, WIDE), F32)],
        )(weights)

    def run(layer, cells, bands, readers=()):
        wide = len(cells) == 3
        final = bool(readers)
        outs = (shaped((8, WIDE), F32),) if final else (shaped((CELLS, channels)),) * (1 + wide)
        return call(
            functools.partial(layer_kernel, layer, len(cells), final),
            outs,
            [VMEM] * (len(cells) + 4 + wide + final),
            [pltpu.VMEM((CELLS, channels), BF16)] * (1 + wide),
        )(*cells, bands[-1], *bands[:-1], *readers, mine, theirs[layer // 2])

    own_cols = own_columns((0, 1), after(mine, taps))
    theirs = [
        core(after(m[:, :528], *tables[::-1], field_core, field_chip, own_cols[0])) for m in (mine[:2],)
    ]

    margin, rows0, rows1 = prepare((0, 1), [after(tables[0], field_chip)] + tables[1:])
    theirs.append(core(after(mine[2:, :528], rows0)))
    cells = run(0, (field, field_core, field_chip), (own_cols[0], margin, rows0))
    (state,) = run(1, cells, (own_cols[1], rows1))
    own_cols = own_columns((2, 3), after(mine, state))
    margin, rows2, rows3 = prepare((2, 3), [after(t, state) for t in tables])
    cells = run(2, (state, core(state), beside(state)), (own_cols[0], margin, rows2))
    (density,) = run(3, cells, (own_cols[1], rows3), (readout.reshape(1, channels),))

    beside_density = core(density)
    pair = jnp.where(c == 0, jnp.stack([density, beside_density]), jnp.stack([beside_density, density]))
    pairs = [chip(pair, k) for k in (3, 2, 1)]
    return call(
        gather_kernel, shaped((1, 4, WIDE), F32), [VMEM] * 4, [pltpu.VMEM((4, 2, 8, WIDE), F32)]
    )(pair, *pairs)


def on_device(raster, row_coef, *rest):
    fits = (
        lax.axis_size("section") == 4
        and lax.axis_size("space") == 8
        and raster.shape == (4, 4, WIDE, 256)
        and row_coef.shape[1] == TAPS
    )
    plan = window_on_section if fits else layers_over_sections
    return plan(raster, row_coef, *rest)


def solution(mesh):
    placed = (
        P(None, "space", None, None),
        P("section", None, "space", None),
        P("section", None, "space", None),
        P("section", None),
        P("section", None, None),
        P("section", None),
        P("section", None, None),
        P(),
    )
    return jax.shard_map(
        on_device,
        mesh=mesh,
        in_specs=placed,
        out_specs=P("section", "space", None),
        check_vma=False,
    )
```

```python
import functools

import jax
import jax.numpy as jnp
from jax import lax
from jax.experimental import pallas as pl
from jax.experimental.pallas import tpu as pltpu
from jax.sharding import PartitionSpec as P

F32 = jnp.float32
BF16 = jnp.bfloat16
VMEM = pl.BlockSpec(memory_space=pltpu.VMEM)
ANY = pl.BlockSpec(memory_space=pl.ANY)


def from_behind(array, axis, by):
    size = lax.axis_size(axis)
    pairs = [(i, i + by) for i in range(size) if 0 <= i + by < size]
    return lax.ppermute(array, axis, pairs)


def from_root(value, axis, source):
    kept = jnp.where(lax.axis_index(axis) == source, value, 0).astype(value.dtype)
    return lax.psum(kept, axis)


def row_stencil(surface, coefficients):
    taps_count = coefficients.shape[0]
    radius = taps_count // 2
    columns = surface.shape[1]
    padded = jnp.pad(surface.astype(F32), ((0, 0), (radius, radius), (0, 0)))
    summed = jnp.zeros(surface.shape, F32)
    for offset in range(taps_count):
        summed = (
            summed
            + coefficients[offset].astype(F32)[:, :, None] * padded[:, offset : offset + columns, :]
        )
    return summed


def col_stencil(surface, coefficients):
    taps_count = coefficients.shape[0]
    radius = taps_count // 2
    lines = surface.shape[0]
    swapped = jnp.swapaxes(coefficients, 1, 2)
    padded = jnp.pad(surface.astype(F32), ((radius, radius), (0, 0), (0, 0)))
    summed = jnp.zeros(surface.shape, F32)
    for offset in range(taps_count):
        summed = (
            summed
            + swapped[offset].astype(F32)[:, :, None] * padded[offset : offset + lines, :, :]
        )
    return summed


def apply_layer(current, params):
    row_part = row_stencil(current, params[0]).astype(BF16)
    columns_view = lax.all_to_all(row_part, "space", split_axis=1, concat_axis=0, tiled=True)
    mixed_field = col_stencil(columns_view, params[1])
    inverse = lax.rsqrt(jnp.mean(mixed_field * mixed_field, axis=-1, keepdims=True) + 1e-06)
    normed = (mixed_field * inverse * params[2].astype(F32)).astype(BF16)
    hidden = jax.nn.gelu(
        jnp.dot(normed, params[3], preferred_element_type=F32) + params[4].astype(F32),
        approximate=True,
    ).astype(BF16)
    return (mixed_field + jnp.dot(hidden, params[5], preferred_element_type=F32)).astype(BF16)


def to_rows(output):
    return lax.all_to_all(output, "space", split_axis=0, concat_axis=1, tiled=True)


def read_density(output, readout):
    return jax.nn.softplus(jnp.dot(output, readout, preferred_element_type=F32))


def layers_over_sections(
    raster, row_coef, col_coef, norm_gain, weight_in, bias_in, weight_out, readout
):
    sections = lax.axis_size("section")
    spaces = lax.axis_size("space")
    windows = raster.shape[0]
    position = lax.axis_index("section")
    params = (row_coef[0], col_coef[0], norm_gain[0], weight_in[0], bias_in[0], weight_out[0])
    carried = jnp.zeros(raster.shape[1:], BF16)
    finished = jnp.zeros((windows, raster.shape[1] * spaces, raster.shape[2] // spaces), F32)
    for moment in range(windows + sections - 1):
        entering = raster[min(moment, windows - 1)]
        current = jnp.where(position == 0, entering, carried)
        output = apply_layer(current, params)
        finished_index = moment - (sections - 1)
        if finished_index >= 0:
            finished = finished.at[finished_index].set(read_density(output, readout))
        if moment < windows + sections - 2:
            carried = from_behind(to_rows(output), "section", 1)
    row_density = lax.all_to_all(finished, "space", split_axis=1, concat_axis=2, tiled=True)
    everyone = from_root(row_density, "section", sections - 1)
    return lax.dynamic_slice_in_dim(everyone, position, 1, 0)


TAPS = 15
RADIUS = 7
ROWS = 32
COLS = 16
WIDE = 128
CELLS = ROWS * COLS
GROUP = 8 * COLS


def call(kernel, outs, specs, scratch=(), room=48, place=VMEM):
    return pl.pallas_call(
        kernel,
        out_shape=outs,
        in_specs=specs,
        out_specs=jax.tree.map(lambda _: place, outs),
        scratch_shapes=list(scratch),
        compiler_params=pltpu.CompilerParams(vmem_limit_bytes=room * 1024 * 1024),
        cost_estimate=pl.CostEstimate(flops=1, bytes_accessed=1, transcendentals=0),
    )


def after(array, *others):
    return lax.optimization_barrier((array, *others))[0]


def shaped(shape, kind=BF16):
    return jax.ShapeDtypeStruct(shape, kind)


def iota(shape, axis):
    return lax.broadcasted_iota(jnp.int32, shape, axis)


def picked(which, values):
    out = values[0]
    for k in range(1, len(values)):
        out = jnp.where(which == k, values[k], out)
    return out


def position():
    s, p = lax.axis_index("section"), lax.axis_index("space")
    return s, p % 2, p // 2, p


def stage_kernel(row_coef, col_coef, weight_in, weight_out, bias, gain, out, own, *scratch):
    rows, cols, biases, gains, half, taps, arrive, leave = scratch
    _, c, _, _ = position()
    start = pl.multiple_of(c * 256, 256)
    copies = [
        pltpu.make_async_copy(row_coef.at[0], rows, arrive.at[0]),
        pltpu.make_async_copy(col_coef.at[0], cols, arrive.at[1]),
        pltpu.make_async_copy(bias, biases, arrive.at[2]),
        pltpu.make_async_copy(gain, gains, arrive.at[3]),
        pltpu.make_async_copy(weight_in.at[0, :, pl.ds(start, 256)], half.at[0:256, :], arrive.at[4]),
        pltpu.make_async_copy(weight_out.at[0, pl.ds(start, 256), :], half.at[256:512, :], arrive.at[5]),
    ]
    for copy in copies:
        copy.start()
    for copy in copies[:4]:
        copy.wait()
    line = iota((16, 256), 0)
    part = jnp.where(c == 0, biases[:, 0:256].astype(F32), biases[:, 256:512].astype(F32))
    tail = jnp.where(line == 0, part, jnp.where(line == 1, gains[...].astype(F32), 0.0))
    half[512:528, :] = tail.astype(BF16)
    zero = jnp.zeros((1, WIDE), F32)
    row, col = rows[...].astype(F32), cols[...].astype(F32)
    for m in range(4):
        taps[m] = jnp.concatenate([row[:, m, :], zero], 0).astype(BF16)
        group = jnp.concatenate([col[:, 4 * m + j, :] for j in range(4)], 1)
        group = jnp.concatenate([group, zero], 0).astype(BF16)
        taps[4 + m] = group
        half[528 + 16 * (m // 2) : 544 + 16 * (m // 2), WIDE * (m % 2) : WIDE * (m % 2 + 1)] = group
    for copy in copies[4:]:
        copy.wait()
    sends = [pltpu.make_async_copy(half, out.at[n], leave.at[n]) for n in range(4)]
    sends.append(pltpu.make_async_copy(taps, own, leave.at[4]))
    for copy in sends:
        copy.start()
    for copy in sends:
        copy.wait()


def chunk_kernel(own_taps, sib_taps, own, sib, o0, o1, o2, o3, chunk):
    _, c, z, _ = position()
    channels = own.shape[-1]
    for i in range(8):
        cells = jnp.where(c == i // 4, own[i % 4], sib[i % 4]).reshape(4, 2, COLS, channels)
        chunk[:, COLS * i : COLS * (i + 1), :] = jnp.where(c == 0, cells[:, 0], cells[:, 1])
    first, second = own_taps[0:4].astype(F32), sib_taps[0:4].astype(F32)
    taps = jnp.concatenate([jnp.where(c == 0, first, second), jnp.where(c == 0, second, first)], 0)
    turned = jnp.transpose(taps.reshape(WIDE, WIDE)).reshape(16, 8, WIDE)
    for to in range(4):
        at = [jnp.where(c == 0, turned[(4 * to + d) % 16], turned[(4 * to + d + 2) % 16]) for d in (-1, 0, 1, 2)]
        sides = [jnp.concatenate([at[1], at[2]], 0), jnp.concatenate([at[0], at[3]], 0)]
        chunk[to, GROUP : GROUP + 16, :] = jnp.concatenate(sides, 1).astype(BF16)
        edge = [jnp.where(c == 0, sib_taps[m + 6], sib_taps[m + 4]) for m in range(2)]
        chunk[to, GROUP + 16 : GROUP + 32, :] = jnp.concatenate(edge, 1)
    for k, out in enumerate((o0, o1, o2, o3)):
        out[...] = chunk[z ^ k, 0 : out.shape[0], :]


def tables_kernel(g0, g3, g2, g1, sib_taps, taps, edges):
    _, c, z, _ = position()
    for k, g in enumerate((g0, g1, g2, g3)):
        taps[16 * k : 16 * (k + 1), :] = g[GROUP : GROUP + 16, :]
        if k != 2:
            edges[z ^ k] = g[GROUP + 16 : GROUP + 32, :]
    chip = edges[(z + 3 + 2 * c) % 4]
    for n in range(2):
        core = jnp.concatenate([sib_taps[4 + (2 * n + m + 2) % 4] for m in range(2)], 1)
        left = c == n
        taps[64 + 16 * n : 80 + 16 * n, :] = jnp.where(left, chip, core)


def field_kernel(g0, g3, g2, g1, field):
    _, _, z, _ = position()
    for k, g in enumerate((g0, g1, g2, g3)):
        field[pl.ds(pl.multiple_of((z ^ k) * GROUP, GROUP), GROUP), :] = g[0:GROUP, :]


def columns(groups, out, turned, ordered):
    tap_in, tap_out = iota((WIDE, 256), 0), iota((WIDE, 256), 1)
    expand = jnp.where((tap_in == tap_out // COLS) & (tap_in < TAPS), 1.0, 0.0).astype(BF16)
    lane, line = iota((COLS, 256), 1), iota((COLS, 256), 0)
    same = line == lane % COLS
    for m, group in enumerate(groups):
        turned[128 * m : 128 * (m + 1), :] = jnp.concatenate(
            [jnp.transpose(group), jnp.zeros((128, WIDE - 16), F32)], 1
        )
    for i in range(ROWS):
        ordered[COLS * i : COLS * (i + 1), :] = turned[pl.ds(i, COLS, stride=ROWS), :]
    wide = jnp.dot(ordered[...].astype(BF16), expand, preferred_element_type=F32)
    for i in range(ROWS):
        row = i + lane // COLS - RADIUS
        block = jnp.where(same & (row >= 0) & (row < ROWS), wide[COLS * i : COLS * (i + 1)], 0.0)
        block = jnp.concatenate([block, jnp.zeros((COLS, CELLS - 256), F32)], 1)
        shift = (COLS * (i - RADIUS)) % CELLS
        if shift:
            block = pltpu.roll(block, shift, 1)
        out[COLS * i : COLS * (i + 1), :] = block.astype(BF16)


def own_columns_kernel(layers, weights, *rest):
    outs, scratch = rest[:-2], rest[-2:]
    for layer, out in zip(layers, outs):
        table = weights[layer, 528:560, :].astype(F32)
        groups = [table[16 * n : 16 * (n + 1), WIDE * m : WIDE * (m + 1)] for n in range(2) for m in range(2)]
        columns(groups, out, *scratch)


def prepare_kernel(layers, last, q0, q3, q2, q1, *rest):
    s, c, z, p = position()
    outs, (turned, ordered, parts) = list(rest[:-3]), rest[-3:]

    lane2, line2 = iota((GROUP, WIDE), 1), iota((GROUP, WIDE), 0)
    tap = (lane2 - line2 + RADIUS + WIDE) % WIDE
    source = line2 % COLS + tap - RADIUS
    inside = (tap < TAPS) & (source >= 0) & (source < COLS)
    on_left = (tap < TAPS) & (source < 0) & (p > 0)
    on_right = (tap < TAPS) & (source >= COLS) & (p < last)
    h = line2 % COLS
    tap_u = (lane2 - line2 - 1 + WIDE) % WIDE
    tap_v = (lane2 - line2 + 15 + WIDE) % WIDE
    u_left = (h < 8) & (tap_u < TAPS) & (h + tap_u < 15)
    u_own = (h >= 8) & (tap_u < TAPS) & (h + tap_u < 15)
    v_own = (h < 8) & (tap_v < TAPS) & (h + tap_v >= 15)
    v_right = (h >= 8) & (tap_v < TAPS) & (h + tap_v >= 15)

    def rolled(part, shift):
        return jnp.concatenate([pltpu.roll(part, shift, 1, stride=1, stride_axis=0)] * 8, 0)

    def sides(left, right):
        first = c == (0 if layer == 0 else 1)
        return jnp.where(first, right, left).astype(BF16), jnp.where(first, left, right).astype(BF16)

    for layer in layers:
        table = picked(s ^ layer, [q[...].astype(F32) for q in (q0, q1, q2, q3)])
        if layer % 2 == 0:
            margin = table[64:96]
            groups = [margin[16 * n : 16 * (n + 1), WIDE * m : WIDE * (m + 1)] for n in range(2) for m in range(2)]
            columns(groups, outs.pop(0), turned, ordered)
        out = outs.pop(0)
        for k in range(4):
            parts[z ^ k] = table[16 * k : 16 * (k + 1)]
        for g in range(4):
            part = parts[g]
            band = rolled(part[:, 0:WIDE], WIDE - RADIUS)
            left, right = jnp.where(on_left, band, 0.0), jnp.where(on_right, band, 0.0)
            out[g, 0:GROUP, 0:WIDE] = jnp.where(inside, band, 0.0).astype(BF16)
            if layer % 2 == 1:
                margin = pltpu.roll(left, 8, 1) + pltpu.roll(right, WIDE - 8, 1)
                out[g, 0:GROUP, WIDE : 2 * WIDE] = margin.astype(BF16)
                continue
            core, chip = sides(pltpu.roll(left, 16, 1), pltpu.roll(right, WIDE - 16, 1))
            out[g, 0:GROUP, WIDE : 2 * WIDE] = core
            out[g, 0:GROUP, 2 * WIDE : 3 * WIDE] = chip
            band = rolled(part[:, WIDE : 2 * WIDE], 1)
            back = pltpu.roll(band, WIDE - 16, 1)
            mid = jnp.where(u_own, band, jnp.where(v_own, back, 0.0))
            core, chip = sides(jnp.where(u_left, band, 0.0), jnp.where(v_right, back, 0.0))
            out[g, GROUP : 2 * GROUP, 0:WIDE] = mid.astype(BF16)
            out[g, GROUP : 2 * GROUP, WIDE : 2 * WIDE] = core
            out[g, GROUP : 2 * GROUP, 2 * WIDE : 3 * WIDE] = chip


def layer_kernel(layer, fields, final, *refs):
    cells, refs = refs[:fields], refs[fields:]
    wide = fields == 3
    bands, refs = refs[0], refs[1:]
    col_bands, refs = refs[: 1 + wide], refs[1 + wide :]
    if final:
        readout, refs = refs[0], refs[1:]
    mine, theirs, refs = refs[0], refs[1], refs[2:]
    outs, rows = refs[: 1 + wide], refs[1 + wide :]
    halves = (mine.at[layer], theirs.at[layer % 2])
    channels = cells[0].shape[-1]
    for g in range(4):
        cut = slice(GROUP * g, GROUP * (g + 1))
        stacked = jnp.concatenate([x[cut] for x in cells], 0)
        done = jnp.dot(bands[g], stacked, preferred_element_type=F32).astype(BF16)
        for n, row in enumerate(rows):
            row[cut, :] = done[GROUP * n : GROUP * (n + 1)]
    size = 512
    mixed = [
        jnp.dot(band[size * b : size * (b + 1), :], row[...], preferred_element_type=F32)
        for band, row in zip(col_bands, rows)
        for b in range(CELLS // size)
    ]
    gain = halves[0][512:528, :].astype(F32)[1:2]
    bias = jnp.concatenate([half[512:528, :].astype(F32)[0:1] for half in halves], 1)
    weight_in = jnp.concatenate([half[0:256, :] for half in halves], 1)
    weight_out = jnp.concatenate([half[256:512, :] for half in halves], 0)
    for n, total in enumerate(mixed):
        inverse = lax.rsqrt(jnp.mean(total * total, axis=-1, keepdims=True) + 1e-06)
        normed = (total * inverse * gain).astype(BF16)
        hidden = jnp.dot(normed, weight_in, preferred_element_type=F32) + bias
        inner = hidden * (0.7978845608028654 + 0.035677408136300125 * (hidden * hidden))
        hidden = (hidden + hidden * jnp.tanh(inner)).astype(BF16)
        total = (total + 0.5 * jnp.dot(hidden, weight_out, preferred_element_type=F32)).astype(BF16)
        out, b = outs[n // (CELLS // size)], n % (CELLS // size)
        if final:
            reader = jnp.broadcast_to(readout[...], (8, channels))
            logit = lax.dot_general(reader, total, (((1,), (1,)), ((), ())), preferred_element_type=F32)
            logit = jnp.maximum(logit, 0.0) + jnp.log1p(jnp.exp(-jnp.abs(logit)))
            for d in range(size // 64):
                moved = pltpu.roll(logit, size - 64 * d, 1) if d else logit
                out[size // 64 * b + d : size // 64 * b + d + 1, :] = moved[0:1, 0:WIDE]
        else:
            out[size * b : size * (b + 1), :] = total


def gather_kernel(g0, g3, g2, g1, out, parts):
    _, _, z, p = position()
    for k, g in enumerate((g0, g1, g2, g3)):
        parts[z ^ k] = g[...]
    lane, line = iota((8, WIDE), 1), iota((8, WIDE), 0)
    mask = lane // COLS == line
    cells = jnp.concatenate([parts[g, core, pl.ds(p, 1), :] for g in range(4) for core in range(2)], 0)
    cells = pltpu.roll(cells, 0, 1, stride=COLS, stride_axis=0)
    for t in range(4):
        moved = pltpu.roll(cells, WIDE - COLS * t, 1) if t else cells
        out[0, t : t + 1, :] = jnp.sum(jnp.where(mask, moved, 0.0), axis=0, keepdims=True)


def window_on_section(raster, row_coef, col_coef, norm_gain, weight_in, bias_in, weight_out, readout):
    c = lax.axis_index("space") % 2
    channels = raster.shape[-1]
    spaces = lax.axis_size("space")

    def core(array):
        return lax.ppermute(array, "space", [(i, i ^ 1) for i in range(spaces)])

    def chip(array, k):
        return lax.ppermute(array, "space", [(i, i ^ (2 * k)) for i in range(spaces)])

    def section(array, k):
        return lax.ppermute(array, "section", [(i, i ^ k) for i in range(4)])

    def beside(array, ends=True):
        pairs = []
        for a in range(4):
            for q in range(spaces):
                other = q - 1 if q % 2 == 0 else q + 1
                to = a * spaces + other if 0 <= other < spaces else (a ^ 1) * spaces + q
                if ends or 0 <= other < spaces:
                    pairs.append((a * spaces + q, to))
        return lax.ppermute(array, ("section", "space"), pairs)

    window = lax.dynamic_index_in_dim(raster, lax.axis_index("section"), 0, keepdims=False)
    window_sib = core(window)
    packed, own = call(
        stage_kernel,
        (shaped((4, 560, 256)), shaped((8, 16, WIDE))),
        [ANY] * 6,
        [
            pltpu.VMEM(row_coef.shape[1:], BF16),
            pltpu.VMEM(col_coef.shape[1:], BF16),
            pltpu.VMEM((1, 512), BF16),
            pltpu.VMEM((1, 256), BF16),
            pltpu.VMEM((560, 256), BF16),
            pltpu.VMEM((8, 16, WIDE), BF16),
            pltpu.SemaphoreType.DMA((6,)),
            pltpu.SemaphoreType.DMA((5,)),
        ],
        room=56,
        place=ANY,
    )(row_coef, col_coef, weight_in, weight_out, bias_in, norm_gain)
    sib = core(own)

    chunks = call(
        chunk_kernel,
        tuple(shaped((GROUP + lines, channels)) for lines in (32, 32, 16, 32)),
        [VMEM] * 4,
        [pltpu.VMEM((4, GROUP + 32, channels), BF16)],
    )(own, sib, window, window_sib)
    sent = chunks
    chunks = [sent[0]] + [chip(sent[k], k) for k in (3, 2, 1)][::-1]

    mine = lax.all_to_all(packed, "section", split_axis=0, concat_axis=0, tiled=True)

    taps = call(
        tables_kernel, shaped((96, 256)), [VMEM] * 5, [pltpu.VMEM((4, 16, 256), BF16)]
    )(chunks[0], *chunks[:0:-1], sib)
    field = call(field_kernel, shaped((CELLS, channels)), [VMEM] * 4)(after(chunks[0], taps), *chunks[:0:-1])
    field_core, field_chip = core(field), beside(field)
    tables = [section(taps, k) for k in (3, 2, 1)]
    tables = [taps] + tables[::-1]
    def prepare(layers, tables):
        outs = []
        for layer in layers:
            even = layer % 2 == 0
            outs += [shaped((CELLS, CELLS))] * even
            outs.append(shaped((4, 2 * GROUP, 3 * WIDE) if even else (4, GROUP, 2 * WIDE)))
        return call(
            functools.partial(prepare_kernel, layers, spaces - 1),
            tuple(outs),
            [VMEM] * 4,
            [pltpu.VMEM((CELLS, WIDE), F32), pltpu.VMEM((CELLS, WIDE), F32), pltpu.VMEM((4, 16, 256), F32)],
        )(tables[0], *tables[:0:-1])

    def own_columns(layers, weights):
        return call(
            functools.partial(own_columns_kernel, layers),
            (shaped((CELLS, CELLS)),) * len(layers),
            [VMEM],
            [pltpu.VMEM((CELLS, WIDE), F32), pltpu.VMEM((CELLS, WIDE), F32)],
        )(weights)

    def run(layer, cells, bands, readers=()):
        wide = len(cells) == 3
        final = bool(readers)
        outs = (shaped((8, WIDE), F32),) if final else (shaped((CELLS, channels)),) * (1 + wide)
        return call(
            functools.partial(layer_kernel, layer, len(cells), final),
            outs,
            [VMEM] * (len(cells) + 4 + wide + final),
            [pltpu.VMEM((CELLS, channels), BF16)] * (1 + wide),
        )(*cells, bands[-1], *bands[:-1], *readers, mine, theirs[layer // 2])

    own_cols = own_columns((0, 1), after(mine, taps))
    theirs = [
        core(after(m[:, :528], *tables[::-1], field_core, field_chip, own_cols[0])) for m in (mine[:2],)
    ]

    margin, rows0, rows1 = prepare((0, 1), [after(tables[0], field_chip)] + tables[1:])
    theirs.append(core(after(mine[2:, :528], rows0)))
    cells = run(0, (field, field_core, field_chip), (own_cols[0], margin, rows0))
    (state,) = run(1, cells, (own_cols[1], rows1))
    own_cols = own_columns((2, 3), after(mine, state))
    margin, rows2, rows3 = prepare((2, 3), [after(t, state) for t in tables])
    cells = run(2, (state, beside(state), core(state)), (own_cols[0], margin, rows2))
    (density,) = run(3, cells, (own_cols[1], rows3), (readout.reshape(1, channels),))

    beside_density = core(density)
    pair = jnp.where(c == 0, jnp.stack([density, beside_density]), jnp.stack([beside_density, density]))
    pairs = [chip(pair, k) for k in (3, 2, 1)]
    return call(
        gather_kernel, shaped((1, 4, WIDE), F32), [VMEM] * 4, [pltpu.VMEM((4, 2, 8, WIDE), F32)]
    )(pair, *pairs)


def on_device(raster, row_coef, *rest):
    fits = (
        lax.axis_size("section") == 4
        and lax.axis_size("space") == 8
        and raster.shape == (4, 4, WIDE, 256)
        and row_coef.shape[1] == TAPS
    )
    plan = window_on_section if fits else layers_over_sections
    return plan(raster, row_coef, *rest)


def solution(mesh):
    placed = (
        P(None, "space", None, None),
        P("section", None, "space", None),
        P("section", None, "space", None),
        P("section", None),
        P("section", None, None),
        P("section", None),
        P("section", None, None),
        P(),
    )
    return jax.shard_map(
        on_device,
        mesh=mesh,
        in_specs=placed,
        out_specs=P("section", "space", None),
        check_vma=False,
    )
```

```python
import functools

import jax
import jax.numpy as jnp
from jax import lax
from jax.experimental import pallas as pl
from jax.experimental.pallas import tpu as pltpu
from jax.sharding import PartitionSpec as P

F32 = jnp.float32
BF16 = jnp.bfloat16
VMEM = pl.BlockSpec(memory_space=pltpu.VMEM)
ANY = pl.BlockSpec(memory_space=pl.ANY)


def from_behind(array, axis, by):
    size = lax.axis_size(axis)
    pairs = [(i, i + by) for i in range(size) if 0 <= i + by < size]
    return lax.ppermute(array, axis, pairs)


def from_root(value, axis, source):
    kept = jnp.where(lax.axis_index(axis) == source, value, 0).astype(value.dtype)
    return lax.psum(kept, axis)


def row_stencil(surface, coefficients):
    taps_count = coefficients.shape[0]
    radius = taps_count // 2
    columns = surface.shape[1]
    padded = jnp.pad(surface.astype(F32), ((0, 0), (radius, radius), (0, 0)))
    summed = jnp.zeros(surface.shape, F32)
    for offset in range(taps_count):
        summed = (
            summed
            + coefficients[offset].astype(F32)[:, :, None] * padded[:, offset : offset + columns, :]
        )
    return summed


def col_stencil(surface, coefficients):
    taps_count = coefficients.shape[0]
    radius = taps_count // 2
    lines = surface.shape[0]
    swapped = jnp.swapaxes(coefficients, 1, 2)
    padded = jnp.pad(surface.astype(F32), ((radius, radius), (0, 0), (0, 0)))
    summed = jnp.zeros(surface.shape, F32)
    for offset in range(taps_count):
        summed = (
            summed
            + swapped[offset].astype(F32)[:, :, None] * padded[offset : offset + lines, :, :]
        )
    return summed


def apply_layer(current, params):
    row_part = row_stencil(current, params[0]).astype(BF16)
    columns_view = lax.all_to_all(row_part, "space", split_axis=1, concat_axis=0, tiled=True)
    mixed_field = col_stencil(columns_view, params[1])
    inverse = lax.rsqrt(jnp.mean(mixed_field * mixed_field, axis=-1, keepdims=True) + 1e-06)
    normed = (mixed_field * inverse * params[2].astype(F32)).astype(BF16)
    hidden = jax.nn.gelu(
        jnp.dot(normed, params[3], preferred_element_type=F32) + params[4].astype(F32),
        approximate=True,
    ).astype(BF16)
    return (mixed_field + jnp.dot(hidden, params[5], preferred_element_type=F32)).astype(BF16)


def to_rows(output):
    return lax.all_to_all(output, "space", split_axis=0, concat_axis=1, tiled=True)


def read_density(output, readout):
    return jax.nn.softplus(jnp.dot(output, readout, preferred_element_type=F32))


def layers_over_sections(
    raster, row_coef, col_coef, norm_gain, weight_in, bias_in, weight_out, readout
):
    sections = lax.axis_size("section")
    spaces = lax.axis_size("space")
    windows = raster.shape[0]
    position = lax.axis_index("section")
    params = (row_coef[0], col_coef[0], norm_gain[0], weight_in[0], bias_in[0], weight_out[0])
    carried = jnp.zeros(raster.shape[1:], BF16)
    finished = jnp.zeros((windows, raster.shape[1] * spaces, raster.shape[2] // spaces), F32)
    for moment in range(windows + sections - 1):
        entering = raster[min(moment, windows - 1)]
        current = jnp.where(position == 0, entering, carried)
        output = apply_layer(current, params)
        finished_index = moment - (sections - 1)
        if finished_index >= 0:
            finished = finished.at[finished_index].set(read_density(output, readout))
        if moment < windows + sections - 2:
            carried = from_behind(to_rows(output), "section", 1)
    row_density = lax.all_to_all(finished, "space", split_axis=1, concat_axis=2, tiled=True)
    everyone = from_root(row_density, "section", sections - 1)
    return lax.dynamic_slice_in_dim(everyone, position, 1, 0)


TAPS = 15
RADIUS = 7
ROWS = 32
COLS = 16
WIDE = 128
CELLS = ROWS * COLS
GROUP = 8 * COLS


def call(kernel, outs, specs, scratch=(), room=48, place=VMEM):
    return pl.pallas_call(
        kernel,
        out_shape=outs,
        in_specs=specs,
        out_specs=jax.tree.map(lambda _: place, outs),
        scratch_shapes=list(scratch),
        compiler_params=pltpu.CompilerParams(vmem_limit_bytes=room * 1024 * 1024),
        cost_estimate=pl.CostEstimate(flops=1, bytes_accessed=1, transcendentals=0),
    )


def after(array, *others):
    return lax.optimization_barrier((array, *others))[0]


def shaped(shape, kind=BF16):
    return jax.ShapeDtypeStruct(shape, kind)


def iota(shape, axis):
    return lax.broadcasted_iota(jnp.int32, shape, axis)


def picked(which, values):
    out = values[0]
    for k in range(1, len(values)):
        out = jnp.where(which == k, values[k], out)
    return out


def position():
    s, p = lax.axis_index("section"), lax.axis_index("space")
    return s, p % 2, p // 2, p


def stage_kernel(row_coef, col_coef, weight_in, weight_out, bias, gain, out, own, *scratch):
    rows, cols, biases, gains, half, taps, arrive, leave = scratch
    _, c, _, _ = position()
    start = pl.multiple_of(c * 256, 256)
    copies = [
        pltpu.make_async_copy(row_coef.at[0], rows, arrive.at[0]),
        pltpu.make_async_copy(col_coef.at[0], cols, arrive.at[1]),
        pltpu.make_async_copy(bias, biases, arrive.at[2]),
        pltpu.make_async_copy(gain, gains, arrive.at[3]),
        pltpu.make_async_copy(weight_in.at[0, :, pl.ds(start, 256)], half.at[0:256, :], arrive.at[4]),
        pltpu.make_async_copy(weight_out.at[0, pl.ds(start, 256), :], half.at[256:512, :], arrive.at[5]),
    ]
    for copy in copies:
        copy.start()
    for copy in copies[:4]:
        copy.wait()
    line = iota((16, 256), 0)
    part = jnp.where(c == 0, biases[:, 0:256].astype(F32), biases[:, 256:512].astype(F32))
    tail = jnp.where(line == 0, part, jnp.where(line == 1, gains[...].astype(F32), 0.0))
    half[512:528, :] = tail.astype(BF16)
    zero = jnp.zeros((1, WIDE), F32)
    row, col = rows[...].astype(F32), cols[...].astype(F32)
    for m in range(4):
        taps[m] = jnp.concatenate([row[:, m, :], zero], 0).astype(BF16)
        group = jnp.concatenate([col[:, 4 * m + j, :] for j in range(4)], 1)
        group = jnp.concatenate([group, zero], 0).astype(BF16)
        taps[4 + m] = group
        half[528 + 16 * (m // 2) : 544 + 16 * (m // 2), WIDE * (m % 2) : WIDE * (m % 2 + 1)] = group
    for copy in copies[4:]:
        copy.wait()
    sends = [pltpu.make_async_copy(half, out.at[n], leave.at[n]) for n in range(4)]
    sends.append(pltpu.make_async_copy(taps, own, leave.at[4]))
    for copy in sends:
        copy.start()
    for copy in sends:
        copy.wait()


def chunk_kernel(own_taps, sib_taps, own, sib, o0, o1, o2, o3, chunk):
    _, c, z, _ = position()
    channels = own.shape[-1]
    for i in range(8):
        cells = jnp.where(c == i // 4, own[i % 4], sib[i % 4]).reshape(4, 2, COLS, channels)
        chunk[:, COLS * i : COLS * (i + 1), :] = jnp.where(c == 0, cells[:, 0], cells[:, 1])
    first, second = own_taps[0:4].astype(F32), sib_taps[0:4].astype(F32)
    taps = jnp.concatenate([jnp.where(c == 0, first, second), jnp.where(c == 0, second, first)], 0)
    turned = jnp.transpose(taps.reshape(WIDE, WIDE)).reshape(16, 8, WIDE)
    for to in range(4):
        at = [jnp.where(c == 0, turned[(4 * to + d) % 16], turned[(4 * to + d + 2) % 16]) for d in (-1, 0, 1, 2)]
        sides = [jnp.concatenate([at[1], at[2]], 0), jnp.concatenate([at[0], at[3]], 0)]
        chunk[to, GROUP : GROUP + 16, :] = jnp.concatenate(sides, 1).astype(BF16)
        edge = [jnp.where(c == 0, sib_taps[m + 6], sib_taps[m + 4]) for m in range(2)]
        chunk[to, GROUP + 16 : GROUP + 32, :] = jnp.concatenate(edge, 1)
    for k, out in enumerate((o0, o1, o2, o3)):
        out[...] = chunk[z ^ k, 0 : out.shape[0], :]


def tables_kernel(g0, g3, g2, g1, sib_taps, taps, edges):
    _, c, z, _ = position()
    for k, g in enumerate((g0, g1, g2, g3)):
        taps[16 * k : 16 * (k + 1), :] = g[GROUP : GROUP + 16, :]
        if k != 2:
            edges[z ^ k] = g[GROUP + 16 : GROUP + 32, :]
    chip = edges[(z + 3 + 2 * c) % 4]
    for n in range(2):
        core = jnp.concatenate([sib_taps[4 + (2 * n + m + 2) % 4] for m in range(2)], 1)
        left = c == n
        taps[64 + 16 * n : 80 + 16 * n, :] = jnp.where(left, chip, core)


def field_kernel(g0, g3, g2, g1, field):
    _, _, z, _ = position()
    for k, g in enumerate((g0, g1, g2, g3)):
        field[pl.ds(pl.multiple_of((z ^ k) * GROUP, GROUP), GROUP), :] = g[0:GROUP, :]


def columns(groups, out, turned, ordered):
    tap_in, tap_out = iota((WIDE, 256), 0), iota((WIDE, 256), 1)
    expand = jnp.where((tap_in == tap_out // COLS) & (tap_in < TAPS), 1.0, 0.0).astype(BF16)
    lane, line = iota((COLS, 256), 1), iota((COLS, 256), 0)
    same = line == lane % COLS
    for m, group in enumerate(groups):
        turned[128 * m : 128 * (m + 1), :] = jnp.concatenate(
            [jnp.transpose(group), jnp.zeros((128, WIDE - 16), F32)], 1
        )
    for i in range(ROWS):
        ordered[COLS * i : COLS * (i + 1), :] = turned[pl.ds(i, COLS, stride=ROWS), :]
    wide = jnp.dot(ordered[...].astype(BF16), expand, preferred_element_type=F32)
    for i in range(ROWS):
        row = i + lane // COLS - RADIUS
        block = jnp.where(same & (row >= 0) & (row < ROWS), wide[COLS * i : COLS * (i + 1)], 0.0)
        block = jnp.concatenate([block, jnp.zeros((COLS, CELLS - 256), F32)], 1)
        shift = (COLS * (i - RADIUS)) % CELLS
        if shift:
            block = pltpu.roll(block, shift, 1)
        out[COLS * i : COLS * (i + 1), :] = block.astype(BF16)


def own_columns_kernel(layers, weights, *rest):
    outs, scratch = rest[:-2], rest[-2:]
    for layer, out in zip(layers, outs):
        table = weights[layer, 528:560, :].astype(F32)
        groups = [table[16 * n : 16 * (n + 1), WIDE * m : WIDE * (m + 1)] for n in range(2) for m in range(2)]
        columns(groups, out, *scratch)


def prepare_kernel(layers, last, q0, q3, q2, q1, *rest):
    s, c, z, p = position()
    outs, (turned, ordered, parts) = list(rest[:-3]), rest[-3:]

    lane2, line2 = iota((GROUP, WIDE), 1), iota((GROUP, WIDE), 0)
    tap = (lane2 - line2 + RADIUS + WIDE) % WIDE
    source = line2 % COLS + tap - RADIUS
    inside = (tap < TAPS) & (source >= 0) & (source < COLS)
    on_left = (tap < TAPS) & (source < 0) & (p > 0)
    on_right = (tap < TAPS) & (source >= COLS) & (p < last)
    h = line2 % COLS
    tap_u = (lane2 - line2 - 1 + WIDE) % WIDE
    tap_v = (lane2 - line2 + 15 + WIDE) % WIDE
    u_left = (h < 8) & (tap_u < TAPS) & (h + tap_u < 15)
    u_own = (h >= 8) & (tap_u < TAPS) & (h + tap_u < 15)
    v_own = (h < 8) & (tap_v < TAPS) & (h + tap_v >= 15)
    v_right = (h >= 8) & (tap_v < TAPS) & (h + tap_v >= 15)

    def rolled(part, shift):
        return jnp.concatenate([pltpu.roll(part, shift, 1, stride=1, stride_axis=0)] * 8, 0)

    def sides(left, right):
        first = c == (0 if layer == 0 else 1)
        return jnp.where(first, right, left).astype(BF16), jnp.where(first, left, right).astype(BF16)

    for layer in layers:
        table = picked(s ^ layer, [q[...].astype(F32) for q in (q0, q1, q2, q3)])
        if layer % 2 == 0:
            margin = table[64:96]
            groups = [margin[16 * n : 16 * (n + 1), WIDE * m : WIDE * (m + 1)] for n in range(2) for m in range(2)]
            columns(groups, outs.pop(0), turned, ordered)
        out = outs.pop(0)
        for k in range(4):
            parts[z ^ k] = table[16 * k : 16 * (k + 1)]
        for g in range(4):
            part = parts[g]
            band = rolled(part[:, 0:WIDE], WIDE - RADIUS)
            left, right = jnp.where(on_left, band, 0.0), jnp.where(on_right, band, 0.0)
            out[g, 0:GROUP, 0:WIDE] = jnp.where(inside, band, 0.0).astype(BF16)
            if layer % 2 == 1:
                margin = pltpu.roll(left, 8, 1) + pltpu.roll(right, WIDE - 8, 1)
                out[g, 0:GROUP, WIDE : 2 * WIDE] = margin.astype(BF16)
                continue
            core, chip = sides(pltpu.roll(left, 16, 1), pltpu.roll(right, WIDE - 16, 1))
            out[g, 0:GROUP, WIDE : 2 * WIDE] = core
            out[g, 0:GROUP, 2 * WIDE : 3 * WIDE] = chip
            band = rolled(part[:, WIDE : 2 * WIDE], 1)
            back = pltpu.roll(band, WIDE - 16, 1)
            mid = jnp.where(u_own, band, jnp.where(v_own, back, 0.0))
            core, chip = sides(jnp.where(u_left, band, 0.0), jnp.where(v_right, back, 0.0))
            out[g, GROUP : 2 * GROUP, 0:WIDE] = mid.astype(BF16)
            out[g, GROUP : 2 * GROUP, WIDE : 2 * WIDE] = core
            out[g, GROUP : 2 * GROUP, 2 * WIDE : 3 * WIDE] = chip


def layer_kernel(layer, fields, final, *refs):
    cells, refs = refs[:fields], refs[fields:]
    wide = fields == 3
    bands, refs = refs[0], refs[1:]
    col_bands, refs = refs[: 1 + wide], refs[1 + wide :]
    if final:
        readout, refs = refs[0], refs[1:]
    mine, theirs, refs = refs[0], refs[1], refs[2:]
    outs, rows = refs[: 1 + wide], refs[1 + wide :]
    halves = (mine.at[layer], theirs.at[layer % 2])
    channels = cells[0].shape[-1]
    for g in range(4):
        cut = slice(GROUP * g, GROUP * (g + 1))
        stacked = jnp.concatenate([x[cut] for x in cells], 0)
        done = jnp.dot(bands[g], stacked, preferred_element_type=F32).astype(BF16)
        for n, row in enumerate(rows):
            row[cut, :] = done[GROUP * n : GROUP * (n + 1)]
    size = 512
    mixed = [
        jnp.dot(band[size * b : size * (b + 1), :], row[...], preferred_element_type=F32)
        for band, row in zip(col_bands, rows)
        for b in range(CELLS // size)
    ]
    gain = halves[0][512:528, :].astype(F32)[1:2]
    bias = jnp.concatenate([half[512:528, :].astype(F32)[0:1] for half in halves], 1)
    weight_in = jnp.concatenate([half[0:256, :] for half in halves], 1)
    weight_out = jnp.concatenate([half[256:512, :] for half in halves], 0)
    for n, total in enumerate(mixed):
        inverse = lax.rsqrt(jnp.mean(total * total, axis=-1, keepdims=True) + 1e-06)
        normed = (total * inverse * gain).astype(BF16)
        hidden = jnp.dot(normed, weight_in, preferred_element_type=F32) + bias
        inner = hidden * (0.7978845608028654 + 0.035677408136300125 * (hidden * hidden))
        hidden = (hidden + hidden * jnp.tanh(inner)).astype(BF16)
        total = (total + 0.5 * jnp.dot(hidden, weight_out, preferred_element_type=F32)).astype(BF16)
        out, b = outs[n // (CELLS // size)], n % (CELLS // size)
        if final:
            reader = jnp.broadcast_to(readout[...], (8, channels))
            logit = lax.dot_general(reader, total, (((1,), (1,)), ((), ())), preferred_element_type=F32)
            logit = jnp.maximum(logit, 0.0) + jnp.log1p(jnp.exp(-jnp.abs(logit)))
            for d in range(size // 64):
                moved = pltpu.roll(logit, size - 64 * d, 1) if d else logit
                out[size // 64 * b + d : size // 64 * b + d + 1, :] = moved[0:1, 0:WIDE]
        else:
            out[size * b : size * (b + 1), :] = total


def gather_kernel(g0, g3, g2, g1, out, parts):
    _, _, z, p = position()
    for k, g in enumerate((g0, g1, g2, g3)):
        parts[z ^ k] = g[...]
    lane, line = iota((8, WIDE), 1), iota((8, WIDE), 0)
    mask = lane // COLS == line
    cells = jnp.concatenate([parts[g, core, pl.ds(p, 1), :] for g in range(4) for core in range(2)], 0)
    cells = pltpu.roll(cells, 0, 1, stride=COLS, stride_axis=0)
    for t in range(4):
        moved = pltpu.roll(cells, WIDE - COLS * t, 1) if t else cells
        out[0, t : t + 1, :] = jnp.sum(jnp.where(mask, moved, 0.0), axis=0, keepdims=True)


def window_on_section(raster, row_coef, col_coef, norm_gain, weight_in, bias_in, weight_out, readout):
    c = lax.axis_index("space") % 2
    channels = raster.shape[-1]
    spaces = lax.axis_size("space")

    def core(array):
        return lax.ppermute(array, "space", [(i, i ^ 1) for i in range(spaces)])

    def chip(array, k):
        return lax.ppermute(array, "space", [(i, i ^ (2 * k)) for i in range(spaces)])

    def section(array, k):
        return lax.ppermute(array, "section", [(i, i ^ k) for i in range(4)])

    def beside(array, ends=True):
        pairs = []
        for a in range(4):
            for q in range(spaces):
                other = q - 1 if q % 2 == 0 else q + 1
                to = a * spaces + other if 0 <= other < spaces else (a ^ 2) * spaces + q
                if ends or 0 <= other < spaces:
                    pairs.append((a * spaces + q, to))
        return lax.ppermute(array, ("section", "space"), pairs)

    window = lax.dynamic_index_in_dim(raster, lax.axis_index("section"), 0, keepdims=False)
    window_sib = core(window)
    packed, own = call(
        stage_kernel,
        (shaped((4, 560, 256)), shaped((8, 16, WIDE))),
        [ANY] * 6,
        [
            pltpu.VMEM(row_coef.shape[1:], BF16),
            pltpu.VMEM(col_coef.shape[1:], BF16),
            pltpu.VMEM((1, 512), BF16),
            pltpu.VMEM((1, 256), BF16),
            pltpu.VMEM((560, 256), BF16),
            pltpu.VMEM((8, 16, WIDE), BF16),
            pltpu.SemaphoreType.DMA((6,)),
            pltpu.SemaphoreType.DMA((5,)),
        ],
        room=56,
        place=ANY,
    )(row_coef, col_coef, weight_in, weight_out, bias_in, norm_gain)
    sib = core(own)

    chunks = call(
        chunk_kernel,
        tuple(shaped((GROUP + lines, channels)) for lines in (32, 32, 16, 32)),
        [VMEM] * 4,
        [pltpu.VMEM((4, GROUP + 32, channels), BF16)],
    )(own, sib, window, window_sib)
    sent = chunks
    chunks = [sent[0]] + [chip(sent[k], k) for k in (3, 2, 1)][::-1]

    mine = lax.all_to_all(packed, "section", split_axis=0, concat_axis=0, tiled=True)

    taps = call(
        tables_kernel, shaped((96, 256)), [VMEM] * 5, [pltpu.VMEM((4, 16, 256), BF16)]
    )(chunks[0], *chunks[:0:-1], sib)
    field = call(field_kernel, shaped((CELLS, channels)), [VMEM] * 4)(after(chunks[0], taps), *chunks[:0:-1])
    field_core, field_chip = core(field), beside(field)
    tables = [section(taps, k) for k in (3, 2, 1)]
    tables = [taps] + tables[::-1]
    def prepare(layers, tables):
        outs = []
        for layer in layers:
            even = layer % 2 == 0
            outs += [shaped((CELLS, CELLS))] * even
            outs.append(shaped((4, 2 * GROUP, 3 * WIDE) if even else (4, GROUP, 2 * WIDE)))
        return call(
            functools.partial(prepare_kernel, layers, spaces - 1),
            tuple(outs),
            [VMEM] * 4,
            [pltpu.VMEM((CELLS, WIDE), F32), pltpu.VMEM((CELLS, WIDE), F32), pltpu.VMEM((4, 16, 256), F32)],
        )(tables[0], *tables[:0:-1])

    def own_columns(layers, weights):
        return call(
            functools.partial(own_columns_kernel, layers),
            (shaped((CELLS, CELLS)),) * len(layers),
            [VMEM],
            [pltpu.VMEM((CELLS, WIDE), F32), pltpu.VMEM((CELLS, WIDE), F32)],
        )(weights)

    def run(layer, cells, bands, readers=()):
        wide = len(cells) == 3
        final = bool(readers)
        outs = (shaped((8, WIDE), F32),) if final else (shaped((CELLS, channels)),) * (1 + wide)
        return call(
            functools.partial(layer_kernel, layer, len(cells), final),
            outs,
            [VMEM] * (len(cells) + 4 + wide + final),
            [pltpu.VMEM((CELLS, channels), BF16)] * (1 + wide),
        )(*cells, bands[-1], *bands[:-1], *readers, mine, theirs[layer // 2])

    own_cols = own_columns((0, 1), after(mine, taps))
    theirs = [
        core(after(m[:, :528], *tables[::-1], field_core, field_chip, own_cols[0])) for m in (mine[:2],)
    ]

    margin, rows0, rows1 = prepare((0, 1), [after(tables[0], field_chip)] + tables[1:])
    theirs.append(core(after(mine[2:, :528], rows0)))
    cells = run(0, (field, field_core, field_chip), (own_cols[0], margin, rows0))
    (state,) = run(1, cells, (own_cols[1], rows1))
    own_cols = own_columns((2, 3), after(mine, state))
    margin, rows2, rows3 = prepare((2, 3), [after(t, state) for t in tables])
    cells = run(2, (state, beside(state), core(state)), (own_cols[0], margin, rows2))
    (density,) = run(3, cells, (own_cols[1], rows3), (readout.reshape(1, channels),))

    beside_density = core(density)
    pair = jnp.where(c == 0, jnp.stack([density, beside_density]), jnp.stack([beside_density, density]))
    pairs = [chip(pair, k) for k in (3, 2, 1)]
    return call(
        gather_kernel, shaped((1, 4, WIDE), F32), [VMEM] * 4, [pltpu.VMEM((4, 2, 8, WIDE), F32)]
    )(pair, *pairs)


def on_device(raster, row_coef, *rest):
    fits = (
        lax.axis_size("section") == 4
        and lax.axis_size("space") == 8
        and raster.shape == (4, 4, WIDE, 256)
        and row_coef.shape[1] == TAPS
    )
    plan = window_on_section if fits else layers_over_sections
    return plan(raster, row_coef, *rest)


def solution(mesh):
    placed = (
        P(None, "space", None, None),
        P("section", None, "space", None),
        P("section", None, "space", None),
        P("section", None),
        P("section", None, None),
        P("section", None),
        P("section", None, None),
        P(),
    )
    return jax.shard_map(
        on_device,
        mesh=mesh,
        in_specs=placed,
        out_specs=P("section", "space", None),
        check_vma=False,
    )
```
